256 devices in a mesh: lat: 16 (over z_hi, x), lev: 16 (over z_lo, y, core).
Axes of the slice: x: 4, y: 4, z: 8 (z_hi: 4, z_lo: 2; z = z_hi * 2 + z_lo), core: 2. Of those that a mesh axis runs over, the one named last changes fastest.
Arguments:
- tracer: float32 [32, 256, 2304], P('lev', 'lat'), may hold values from 0.5 to 2
- thickness: float32 [32, 256, 2304], P('lev', 'lat'), may hold values from 0.5 to 1.5
- wind_u: float32 [32, 256, 2304], P('lev', 'lat'), may hold values from -4 to 4
- wind_v: float32 [32, 256, 2304], P('lev', 'lat'), may hold values from -4 to 4
- offsets: int32 [32, 256, 2304], P(None, 'lat', 'lev'), may hold values from 0 to 2
- coupling: float32 [31, 256, 2304], P(None, 'lat', 'lev'), may hold values from 0.1 to 10
Outputs:
- tracer_out: float32 [32, 256, 2304], P('lev', 'lat')
- wind_u_out: float32 [32, 256, 2304], P('lev', 'lat')
- wind_v_out: float32 [32, 256, 2304], P('lev', 'lat')
The draws below stay inside these ranges and needn't reach their ends.
All inputs are finite; a program needn't handle non-finite values.
Results may differ from the reference program's by a relative error of at most 0.00002.
Values sent between devices are 32-bit elements; how exact they have to be, the bound alone decides.
No kernel may reach another device: no remote copies, remote signals or barrier semaphores. Data moves between devices by JAX's collectives and lax.ppermute only.
A program may use at most 64 MiB of HBM per device.

```python
import math
import jax
import jax.numpy as jnp

IM = 2304
KM = 32
JM = 256


def with_ends(drawn, stream_key, low, high):
    longest = drawn.shape.index(max(drawn.shape))
    spots = []
    for shift in (0, 1):
        where = [jax.random.randint(jax.random.fold_in(stream_key, axis), (), 0, length) for axis, length in enumerate(drawn.shape)]
        where[longest] = (where[longest] + shift) % drawn.shape[longest]
        spots.append(tuple(where))
    return drawn.at[spots[0]].set(low).at[spots[1]].set(high)


def shard_levels(own_key, extent, cuts, smallest, high):
    def one(axis_at, shards_of):
        steps = jax.random.uniform(jax.random.fold_in(jax.random.fold_in(own_key, 6), axis_at), (shards_of,), jnp.float32, smallest / len(cuts), high / len(cuts))
        return jnp.repeat(jnp.exp(steps), extent[axis_at] // shards_of).reshape((-1,) + (1,) * (len(extent) - axis_at - 1))

    level = one(*cuts[0])
    for cut in cuts[1:]:
        level = level * one(*cut)
    return level


def gaussian(rng, dims, scale, most, cuts=(), held_as=jnp.bfloat16):
    values = scale * jax.random.normal(rng, dims, jnp.float32)
    if cuts:
        values = values * shard_levels(rng, dims, cuts, -0.22, 0.18)
    return jnp.clip(values, -most, most).astype(held_as)


def setup_inputs(seed: int = 0) -> dict:
    key_list = jax.random.split(jax.random.key(seed), 7)
    tracer = jnp.clip(jnp.exp(math.log(2.0) - 1.3862944 * jax.random.uniform(key_list[0], (KM, JM, IM), jnp.float32) ** shard_levels(key_list[0], (KM, JM, IM), ((0, 16), (1, 16)), -0.2, 0.2)), 0.5, 2.0)
    thickness = jnp.clip(0.5 + 1.0 * jax.random.uniform(key_list[1], (KM, JM, IM), jnp.float32) ** shard_levels(key_list[1], (KM, JM, IM), ((0, 16), (1, 16)), -0.2, 0.2), 0.5, 1.5)
    wind_u = gaussian(key_list[2], (KM, JM, IM), 1.0, 4.0, ((0, 16), (1, 16)), jnp.float32)
    wind_v = gaussian(key_list[3], (KM, JM, IM), 1.0, 4.0, ((0, 16), (1, 16)), jnp.float32)
    offsets = with_ends(jax.random.randint(key_list[4], (KM, JM, IM), 0, 3), jax.random.fold_in(key_list[4], 1), 0, 2).astype(jnp.int32)
    coupling = jnp.clip(jnp.exp(math.log(10.0) - 4.6051702 * jax.random.uniform(key_list[5], (KM - 1, JM, IM), jnp.float32) ** shard_levels(key_list[5], (KM - 1, JM, IM), ((1, 16), (2, 16)), -0.2, 0.2)), 0.1, 10.0)
    return dict(tracer=tracer, thickness=thickness, wind_u=wind_u, wind_v=wind_v, offsets=offsets, coupling=coupling)


courant_max = 0.24


def upwind_update(field, east_courant, north_courant):
    west_field = jnp.roll(field, 1, axis=2)
    east_flux = jnp.maximum(east_courant, 0.0) * west_field + jnp.minimum(east_courant, 0.0) * field
    zonal = east_flux - jnp.roll(east_flux, -1, axis=2)
    north_flux = jnp.maximum(north_courant, 0.0) * field[:, :-1] + jnp.minimum(north_courant, 0.0) * field[:, 1:]
    border = jnp.zeros_like(field[:, :1])
    north_flux = jnp.concatenate([border, north_flux, border], axis=1)
    return field + zonal + north_flux[:, :-1] - north_flux[:, 1:]


def column_physics(layer_mass, tracer_mass, east_wind, north_wind, offsets, coupling):
    levels = layer_mass.shape[0]

    def pair_sums(values):
        return [values[k] + values[k + 1] for k in range(levels - 1)]

    def picked(sums, level):
        below_sum = sums[max(level - 1, 0)]
        here_sum = sums[min(level, levels - 2)]
        above_sum = sums[min(level + 1, levels - 2)]
        choose = offsets[level]
        return jnp.where(choose == 0, below_sum, jnp.where(choose == 1, here_sum, above_sum))

    layer_levels = [layer_mass[k] for k in range(levels)]
    layer_sums = pair_sums(layer_levels)
    tracer_sums = pair_sums([tracer_mass[k] for k in range(levels)])
    east_sums = pair_sums([layer_levels[k] * east_wind[k] for k in range(levels)])
    north_sums = pair_sums([layer_levels[k] * north_wind[k] for k in range(levels)])
    zeros = jnp.zeros_like(coupling[0])
    ratio_prev = zeros
    solve_prev = [zeros, zeros, zeros]
    ratios = []
    solves = []
    for level in range(levels):
        total = picked(layer_sums, level)
        rhs = [picked(tracer_sums, level) / total, picked(east_sums, level) / total, picked(north_sums, level) / total]
        low = coupling[level - 1] if level > 0 else zeros
        high = coupling[level] if level < levels - 1 else zeros
        centre = 1.0 + low + high
        denom = centre + low * ratio_prev
        ratio = -high / denom
        solve_now = [(rhs[f] + low * solve_prev[f]) / denom for f in range(3)]
        ratios.append(ratio)
        solves.append(solve_now)
        ratio_prev = ratio
        solve_prev = solve_now
    upper = [zeros, zeros, zeros]
    values = [None] * levels
    for level in range(levels - 1, -1, -1):
        upper = [solves[level][f] - ratios[level] * upper[f] for f in range(3)]
        values[level] = upper
    return tuple(jnp.stack([values[k][f] for k in range(levels)], axis=0) for f in range(3))


def reference(tracer, thickness, wind_u, wind_v, offsets, coupling):
    east_courant = courant_max * jnp.tanh(0.5 * (jnp.roll(wind_u, 1, axis=2) + wind_u))
    north_courant = courant_max * jnp.tanh(0.5 * (wind_v[:, :-1] + wind_v[:, 1:]))
    layer_mass = thickness
    tracer_mass = tracer * thickness
    for substep in range(2):
        layer_mass, tracer_mass = (upwind_update(layer_mass, east_courant, north_courant), upwind_update(tracer_mass, east_courant, north_courant))
    result = column_physics(layer_mass, tracer_mass, wind_u, wind_v, offsets, coupling)
    return (result[0], result[1], result[2])
```

```python
import jax
import jax.numpy as jnp
from jax import lax
from jax.experimental import pallas as pl
from jax.experimental.pallas import tpu as pltpu
from jax.sharding import PartitionSpec as P

courant_max = 0.24
LEVELS = 32
LON = 2304
ROWS = 16
DEST = 16
COLS = 144
LANES = 128
VM = pl.BlockSpec(memory_space=pltpu.VMEM)
SM = pl.BlockSpec(memory_space=pltpu.SMEM)
PARAMS = pltpu.CompilerParams(vmem_limit_bytes=24 * 1024 * 1024)


def lane_ids(rows):
    return lax.broadcasted_iota(jnp.int32, (rows, LANES), 1)


def row_ids(rows):
    return lax.broadcasted_iota(jnp.int32, (rows, LON), 0)


def courant(pair_sum):
    return courant_max * jnp.tanh(0.5 * pair_sum)


def upwind(flow, before, after):
    return jnp.maximum(flow, 0.0) * before + jnp.minimum(flow, 0.0) * after


def east_roll(x):
    return pltpu.roll(x, 1, 1)


def west_roll(x):
    return pltpu.roll(x, LON - 1, 1)


def zonal(east, mass):
    flux = upwind(east, east_roll(mass), mass)
    return flux - west_roll(flux)


def edge_kernel(tracer, thickness, wind_u, wind_v, to_north, to_south):
    def edges(ref):
        return jnp.concatenate(
            [ref[0, 0:2], ref[0, 14:16], ref[1, 0:2], ref[1, 14:16]], axis=0
        )

    u, v, layer = edges(wind_u), edges(wind_v), edges(thickness)
    mass = edges(tracer) * layer
    east = courant(east_roll(u) + u)
    north = courant(v + pltpu.roll(v, 7, 0))
    odd = lax.rem(row_ids(8), 2) == 1

    def partial(m):
        flux = upwind(north, m, pltpu.roll(m, 7, 0))
        return m + zonal(east, m) + jnp.where(odd, pltpu.roll(flux, 1, 0), -flux)

    for slot, value in enumerate((v, layer, mass, partial(layer), partial(mass))):
        for level in range(2):
            to_south[slot, level : level + 1, :] = value[4 * level : 4 * level + 1]
            to_north[slot, level : level + 1, :] = value[4 * level + 3 : 4 * level + 4]


def first_kernel(tracer, thickness, wind_u, wind_v, east_out, north_out, layer_out, mass_out):
    row = row_ids(ROWS)
    for level in range(2):
        u, v, layer = wind_u[level], wind_v[level], thickness[level]
        mass = tracer[level] * layer
        east = courant(east_roll(u) + u)
        north = jnp.where(row == 0, 0.0, courant(pltpu.roll(v, 1, 0) + v))
        east_out[level] = east
        north_out[level] = north
        for m, out in ((layer, layer_out), (mass, mass_out)):
            flux = upwind(north, pltpu.roll(m, 1, 0), m)
            above = jnp.where(row == ROWS - 1, 0.0, pltpu.roll(flux, ROWS - 1, 0))
            out[level] = m + zonal(east, m) + flux - above


def second_kernel(
    inside, tracer, thickness, wind_u, wind_v, east_in, north_in, layer_in, mass_in, south, north_halo, send, held
):
    row = row_ids(ROWS)
    first, last = row == 0, row == ROWS - 1
    for level in range(2):
        east = east_in[level]

        def south_row(slot):
            return south[slot, level : level + 1, :]

        def north_row(slot):
            return north_halo[slot, level : level + 1, :]

        v_low, v_high = wind_v[level, 0:1], wind_v[level, ROWS - 1 : ROWS]
        flow_low = inside[0] * courant(south_row(0) + v_low)
        flow_high = inside[1] * courant(v_high + north_row(0))
        north = jnp.where(first, flow_low, north_in[level])
        layer_low, layer_high = thickness[level, 0:1], thickness[level, ROWS - 1 : ROWS]
        mass_low = tracer[level, 0:1] * layer_low
        mass_high = tracer[level, ROWS - 1 : ROWS] * layer_high
        done = []
        for slot, low, high, partial in (
            (1, layer_low, layer_high, layer_in),
            (2, mass_low, mass_high, mass_in),
        ):
            flux_low = upwind(flow_low, south_row(slot), low)
            flux_high = upwind(flow_high, high, north_row(slot))
            m = partial[level] + jnp.where(first, flux_low, 0.0) - jnp.where(last, flux_high, 0.0)
            m_south = south_row(slot + 2) - flux_low
            m_north = north_row(slot + 2) + flux_high
            flux = upwind(north, jnp.where(first, m_south, pltpu.roll(m, 1, 0)), m)
            top = upwind(flow_high, m[ROWS - 1 : ROWS], m_north)
            above = jnp.where(last, top, pltpu.roll(flux, ROWS - 1, 0))
            done.append(m + zonal(east, m) + flux - above)
        layer, mass = done
        held[0, level] = mass
        held[1, level] = layer * wind_u[level]
        held[2, level] = layer * wind_v[level]
        held[3, level] = layer
    lane = lane_ids(ROWS)
    lane8 = lane_ids(8)
    for dest in range(DEST):
        tile = dest + dest // 8
        shift = 16 * (dest % 8)
        low = slice(tile * LANES, (tile + 1) * LANES)
        high = slice((tile + 1) * LANES, (tile + 2) * LANES)
        for level in range(2):
            packed = None
            for field in range(4):
                here = held[field, level, :, low]
                after = held[field, level, :, high]
                block = here if shift == 0 else jnp.where(lane >= shift, here, after)
                start = (field * 2 + level) * ROWS
                send[dest, start : start + ROWS, :] = block
                for half in range(2):
                    place = 32 * field + 16 * half
                    part = pltpu.roll(after[8 * half : 8 * half + 8], (place - shift) % LANES, 1)
                    packed = part if packed is None else jnp.where(lane8 >= place, part, packed)
            send[dest, 128 + 8 * level : 136 + 8 * level, :] = packed


def factor_kernel(shift_ref, offsets, coupling, choose_main, choose_rest, factors_main, factors_rest):
    shift = shift_ref[0]

    def main(ref, k):
        return pltpu.roll(ref[k, :, 0:LANES], shift, 1)

    def rest(ref, k):
        part = ref[k, :, LANES:COLS]
        both = jnp.concatenate([part[0:8], part[8:16]], axis=1)
        return jnp.concatenate([both, both, both, both], axis=1)

    for load, choose, factors, shape in (
        (main, choose_main, factors_main, (ROWS, LANES)),
        (rest, choose_rest, factors_rest, (8, LANES)),
    ):
        low = jnp.zeros(shape, jnp.float32)
        back = jnp.zeros(shape, jnp.float32)
        for k in range(LEVELS):
            choose[k] = load(offsets, k)
            high = load(coupling, k) if k < LEVELS - 1 else jnp.zeros(shape, jnp.float32)
            scale = 1.0 / (1.0 + low + high - low * back)
            back = high * scale
            factors[0, k] = scale
            factors[1, k] = low * scale
            factors[2, k] = back
            low = high


def column_kernel(received, choose_main, choose_rest, factors_main, factors_rest, send):
    lane = lane_ids(8)

    def main(k):
        base = (k % 2) * ROWS
        return [received[k // 2, base + 32 * f : base + 32 * f + ROWS, :] for f in range(4)]

    def rest(k):
        base = 128 + 8 * (k % 2)
        return received[k // 2, base : base + 8, :]

    def picked(choose, sums):
        return jnp.where(choose == 0, sums[0], jnp.where(choose == 1, sums[1], sums[2]))

    solve_main = [jnp.zeros((ROWS, LANES), jnp.float32)] * 3
    solve_rest = jnp.zeros((8, LANES), jnp.float32)
    main_here, rest_here = main(0), rest(0)
    main_sums, rest_sums = [], []

    def push(k):
        nonlocal main_here, rest_here
        main_next, rest_next = main(k + 1), rest(k + 1)
        main_sums.append([a + b for a, b in zip(main_here, main_next)])
        rest_sums.append(rest_here + rest_next)
        main_here, rest_here = main_next, rest_next

    push(0)
    for k in range(LEVELS):
        if k + 1 < LEVELS - 1:
            push(k + 1)
        three = [max(k - 1, 0), min(k, LEVELS - 2), min(k + 1, LEVELS - 2)]
        choose = choose_main[k]
        values = [picked(choose, [main_sums[i][f] for i in three]) for f in range(4)]
        weight = factors_main[0, k] / values[3]
        low = factors_main[1, k]
        solve_main = [values[f] * weight + low * solve_main[f] for f in range(3)]
        for f in range(3):
            base = (f * 2 + k % 2) * ROWS
            send[k // 2, base : base + ROWS, :] = solve_main[f]
        value = picked(choose_rest[k], [rest_sums[i] for i in three])
        total = jnp.where(lane >= 64, pltpu.roll(value, 96, 1), pltpu.roll(value, 32, 1))
        total = jnp.where(lane >= 32, jnp.where(lane >= 64, total, pltpu.roll(value, 64, 1)), total)
        solve_rest = value * (factors_rest[0, k] / total) + factors_rest[1, k] * solve_rest
        base = 96 + 8 * (k % 2)
        send[k // 2, base : base + 8, :] = solve_rest
    for k in range(LEVELS - 2, -1, -1):
        back = factors_main[2, k]
        for f in range(3):
            base = (f * 2 + k % 2) * ROWS
            solve_main[f] = send[k // 2, base : base + ROWS, :] + back * solve_main[f]
            send[k // 2, base : base + ROWS, :] = solve_main[f]
        base = 96 + 8 * (k % 2)
        solve_rest = send[k // 2, base : base + 8, :] + factors_rest[2, k] * solve_rest
        send[k // 2, base : base + 8, :] = solve_rest


def unpack_kernel(received, tracer_out, u_out, v_out):
    lane = lane_ids(ROWS)
    lane8 = lane_ids(8)
    for level in range(2):
        for field, out in enumerate((tracer_out, u_out, v_out)):
            base = (field * 2 + level) * ROWS
            before = None
            for tile in range(LON // LANES):
                source = tile if tile < 8 else tile - 1
                fresh = tile != 8 and tile != 17
                shift = 16 * (source % 8) if fresh else LANES
                value = received[source, base : base + ROWS, :] if fresh else None
                if shift > 0:
                    last = source - 1 if fresh else (7 if tile == 8 else 15)
                    place = shift - 16
                    packed = received[last, 96 + 8 * level : 104 + 8 * level, :]
                    rest = jnp.concatenate(
                        [
                            pltpu.roll(packed, (place - 32 * field - 16 * half) % LANES, 1)
                            for half in range(2)
                        ],
                        axis=0,
                    )
                    old = received[last, base : base + ROWS, :]
                    old = jnp.where(lane >= place, rest, old) if place > 0 else rest
                    value = jnp.where(lane >= shift, value, old) if fresh else old
                out[level, :, tile * LANES : (tile + 1) * LANES] = value


def call(kernel, in_specs, shapes, scratch=(), flops=1000000, nbytes=3000000):
    return pl.pallas_call(
        kernel,
        in_specs=in_specs,
        out_specs=[VM] * len(shapes),
        out_shape=[jax.ShapeDtypeStruct(s, d) for s, d in shapes],
        scratch_shapes=scratch,
        compiler_params=PARAMS,
        cost_estimate=pl.CostEstimate(flops=flops, bytes_accessed=nbytes, transcendentals=0),
    )


def local(tracer, thickness, wind_u, wind_v, offsets, coupling):
    f32, i32 = jnp.float32, jnp.int32
    lat, lev = lax.axis_index("lat"), lax.axis_index("lev")
    lat_count = lax.axis_size("lat")
    slab = (2, ROWS, LON)
    halo = (5, 2, LON)
    winds = (tracer, thickness, wind_u, wind_v)
    to_north, to_south = call(edge_kernel, [VM] * 4, [(halo, f32)] * 2)(*winds)
    up = [(i, i + 1) for i in range(lat_count - 1)]
    south = lax.ppermute(to_north, "lat", up)
    north = lax.ppermute(to_south, "lat", [(b, a) for a, b in up])
    firsts = call(first_kernel, [VM] * 4, [(slab, f32)] * 4)(*winds)
    inside = jnp.stack([lat > 0, lat < lat_count - 1]).astype(f32)
    (send,) = call(
        second_kernel,
        [SM] + [VM] * 10,
        [((DEST, 144, LANES), f32)],
        scratch=[pltpu.VMEM((4,) + slab, f32)],
    )(inside, *winds, *firsts, south, north)
    received = lax.all_to_all(send, "lev", split_axis=0, concat_axis=0, tiled=True)
    shift = (16 * lax.rem(lev, 8)).astype(i32).reshape(1)
    factors = call(
        factor_kernel,
        [SM, VM, VM],
        [
            ((LEVELS, ROWS, LANES), i32),
            ((LEVELS, 8, LANES), i32),
            ((3, LEVELS, ROWS, LANES), f32),
            ((3, LEVELS, 8, LANES), f32),
        ],
    )(shift, offsets, coupling)
    (back,) = call(column_kernel, [VM] * 5, [((DEST, 112, LANES), f32)])(received, *factors)
    returned = lax.all_to_all(back, "lev", split_axis=0, concat_axis=0, tiled=True)
    return tuple(call(unpack_kernel, [VM], [(slab, f32)] * 3)(returned))


def solution(mesh):
    return jax.shard_map(
        local,
        mesh=mesh,
        in_specs=(
            P("lev", "lat", None),
            P("lev", "lat", None),
            P("lev", "lat", None),
            P("lev", "lat", None),
            P(None, "lat", "lev"),
            P(None, "lat", "lev"),
        ),
        out_specs=(P("lev", "lat", None), P("lev", "lat", None), P("lev", "lat", None)),
        check_vma=False,
    )
```

```python
import jax
import jax.numpy as jnp
from jax import lax
from jax.experimental import pallas as pl
from jax.experimental.pallas import tpu as pltpu
from jax.sharding import PartitionSpec as P

courant_max = 0.24
LEVELS = 32
LON = 2304
ROWS = 16
DEST = 16
COLS = 144
LANES = 128
VM = pl.BlockSpec(memory_space=pltpu.VMEM)
ANY = pl.BlockSpec(memory_space=pl.ANY)
HB = pl.BlockSpec(memory_space=pltpu.HBM)
PARAMS = pltpu.CompilerParams(vmem_limit_bytes=24 * 1024 * 1024)


def lane_ids(rows):
    return lax.broadcasted_iota(jnp.int32, (rows, LANES), 1)


def row_ids(rows):
    return lax.broadcasted_iota(jnp.int32, (rows, LON), 0)


def courant(pair_sum):
    return courant_max * jnp.tanh(0.5 * pair_sum)


def upwind(flow, before, after):
    return jnp.maximum(flow, 0.0) * before + jnp.minimum(flow, 0.0) * after


def east_roll(x):
    return pltpu.roll(x, 1, 1)


def west_roll(x):
    return pltpu.roll(x, LON - 1, 1)


def zonal(east, mass):
    flux = upwind(east, east_roll(mass), mass)
    return flux - west_roll(flux)


def edge_kernel(tracer, thickness, wind_u, wind_v, to_first, to_second, kept, fetched, sems):
    copies = []
    for slot, ref in enumerate((tracer, thickness, wind_u, wind_v)):
        for level in range(2):
            for end in range(2):
                copies.append(
                    pltpu.make_async_copy(
                        ref.at[level, pl.ds(14 * end, 2), :],
                        fetched.at[slot, pl.ds(4 * level + 2 * end, 2), :],
                        sems.at[4 * slot + 2 * level + end],
                    )
                )
    for copy in copies:
        copy.start()
    for copy in copies:
        copy.wait()
    layer, u, v = fetched[1], fetched[2], fetched[3]
    mass = fetched[0] * layer
    east = courant(east_roll(u) + u)
    north = courant(v + pltpu.roll(v, 7, 0))
    odd = lax.rem(row_ids(8), 2) == 1
    upper = lax.rem(row_ids(8), 4) >= 2
    inner = jnp.where(odd, pltpu.roll(north, 1, 0), north)

    def partial(m):
        flux = upwind(north, m, pltpu.roll(m, 7, 0))
        return m + zonal(east, m) + jnp.where(odd, pltpu.roll(flux, 1, 0), -flux)

    values = (v, layer, mass, partial(layer), partial(mass))
    odd_lat = lax.rem(lax.axis_index("lat"), 2) == 1
    north_first = jnp.broadcast_to(odd_lat, (1, LON))
    for slot, value in enumerate(values):
        for level in range(2):
            south = value[4 * level : 4 * level + 1]
            north_row = value[4 * level + 3 : 4 * level + 4]
            to_first[slot, level : level + 1, :] = jnp.where(north_first, north_row, south)
            to_second[slot, level : level + 1, :] = jnp.where(north_first, south, north_row)
        kept[slot] = value
    kept[5] = east
    kept[6] = jnp.where(upper, jnp.minimum(inner, 0.0), -jnp.maximum(inner, 0.0))
    kept[7] = u


def first_kernel(tracer, thickness, wind_u, wind_v, send, edges, held, packed_all, sems):
    row = row_ids(ROWS)
    for level in range(2):
        u, v, layer = wind_u[level], wind_v[level], thickness[level]
        mass = tracer[level] * layer
        east = courant(east_roll(u) + u)
        north = jnp.where(row == 0, 0.0, courant(pltpu.roll(v, 1, 0) + v))
        done = []
        for m in (layer, mass):
            for substep in range(2):
                flux = upwind(north, pltpu.roll(m, 1, 0), m)
                above = jnp.where(row == ROWS - 1, 0.0, pltpu.roll(flux, ROWS - 1, 0))
                m = m + zonal(east, m) + flux - above
            done.append(m)
        layer, mass = done
        for slot, m in enumerate(done):
            edges[slot, 4 * level : 4 * level + 2, :] = m[0:2]
            edges[slot, 4 * level + 2 : 4 * level + 4, :] = m[14:16]
        held[0, level] = mass
        held[1, level] = layer * u
        held[2, level] = layer * v
        held[3, level] = layer
    lane = lane_ids(ROWS)
    lane8 = lane_ids(8)
    copies = []
    for dest in range(DEST):
        tile = dest + dest // 8
        shift = 16 * (dest % 8)
        low = slice(tile * LANES, (tile + 1) * LANES)
        high = slice((tile + 1) * LANES, (tile + 2) * LANES)
        for level in range(2):
            packed = None
            for field in range(4):
                here = held[field, level, :, low]
                after = held[field, level, :, high]
                block = here if shift == 0 else jnp.where(lane >= shift, here, after)
                start = (field * 2 + level) * ROWS
                packed_all[dest, start : start + ROWS, :] = block
                for half in range(2):
                    part = after[8 * half : 8 * half + 8]
                    part = pltpu.roll(part, 2, 0) if half else part
                    place = 32 * field + 16 * half
                    part = pltpu.roll(part, (place - shift) % LANES, 1)
                    packed = part if packed is None else jnp.where(lane8 >= place, part, packed)
            packed_all[dest, 128 + 8 * level : 136 + 8 * level, :] = packed
        copy = pltpu.make_async_copy(packed_all.at[dest], send.at[dest], sems.at[dest])
        copy.start()
        copies.append(copy)
    for copy in copies:
        copy.wait()


def second_kernel(first_halo, second_halo, kept, edges, sent, send, held, patch, sems):
    lat = lax.axis_index("lat")
    row = lax.rem(row_ids(8), 4)
    upper = row >= 2
    outer = (row == 0) | (row == 3)
    even = jnp.broadcast_to(lax.rem(lat, 2) == 0, (1, LON))
    south_open = jnp.where(lat > 0, 1.0, 0.0)
    north_open = jnp.where(lat < lax.axis_size("lat") - 1, 1.0, 0.0)
    open_face = jnp.where(upper, north_open, south_open)

    def halo(slot):
        rows = []
        for level in range(2):
            one = first_halo[slot, level : level + 1, :]
            two = second_halo[slot, level : level + 1, :]
            south = jnp.where(even, one, two)
            north = jnp.where(even, two, one)
            rows.append(jnp.where(upper[0:4], north, south))
        return jnp.concatenate(rows, axis=0)

    v, east, inner = kept[0], kept[5], kept[6]
    flow = open_face * courant(v + halo(0))
    sign = jnp.where(upper, -1.0, 1.0)
    done = []
    for slot in range(2):
        m, m_beyond = kept[1 + slot], halo(1 + slot)
        partial, beyond = kept[3 + slot], halo(3 + slot)
        flux = upwind(flow, jnp.where(upper, m, m_beyond), jnp.where(upper, m_beyond, m))
        change = jnp.where(outer, sign * flux, 0.0)
        partial = partial + change
        beyond = beyond - change
        flux = upwind(flow, jnp.where(upper, partial, beyond), jnp.where(upper, beyond, partial))
        carried = inner * change
        gain = change + zonal(east, change) + carried + sign * flux
        passed = jnp.where(row == 1, pltpu.roll(carried, 1, 0), pltpu.roll(carried, 7, 0))
        done.append(edges[slot] + jnp.where(outer, gain, -passed))
    layer, mass = done
    held[0] = mass
    held[1] = layer * kept[7]
    held[2] = layer * v
    held[3] = layer
    lane = lane_ids(8)
    group = lax.rem(lane, 32) < 16
    for dest in range(DEST):
        tile = dest + dest // 8
        shift = 16 * (dest % 8)
        low = slice(tile * LANES, (tile + 1) * LANES)
        high = slice((tile + 1) * LANES, (tile + 2) * LANES)
        packed = None
        for field in range(4):
            here, after = held[field, :, low], held[field, :, high]
            block = here if shift == 0 else jnp.where(lane >= shift, here, after)
            for level in range(2):
                start = (field * 2 + level) * ROWS
                patch[dest, start : start + 2, :] = block[4 * level : 4 * level + 2]
                patch[dest, start + 14 : start + 16, :] = block[4 * level + 2 : 4 * level + 4]
            place = 32 * field
            both = jnp.where(
                group,
                pltpu.roll(after, (place - shift) % LANES, 1),
                pltpu.roll(pltpu.roll(after, 6, 0), (place + 16 - shift) % LANES, 1),
            )
            packed = both if field == 0 else jnp.where(lane >= place, both, packed)
        for level in range(2):
            start = 128 + 8 * level
            patch[dest, start : start + 2, :] = packed[4 * level : 4 * level + 2]
    spots = [16 * i + end for i in range(8) for end in (0, 14)] + [128, 136]
    copies = [
        pltpu.make_async_copy(
            patch.at[:, pl.ds(spot, 2), :], send.at[:, pl.ds(spot, 2), :], sems.at[i]
        )
        for i, spot in enumerate(spots)
    ]
    for copy in copies:
        copy.start()
    for copy in copies:
        copy.wait()


def factor_kernel(offsets, coupling, factors_main, factors_rest):
    shift = 16 * lax.rem(lax.axis_index("lev"), 8)
    half = lax.rem(lane_ids(8), 32) >= 16

    def main(ref, k):
        return pltpu.roll(ref[k, :, 0:LANES], shift, 1)

    def rest(ref, k):
        part = ref[k, :, LANES:COLS]
        both = jnp.concatenate([part[0:8], part[8:16]], axis=1)
        all_fields = jnp.concatenate([both, both, both, both], axis=1)
        return jnp.where(half, pltpu.roll(all_fields, 2, 0), all_fields)

    for load, factors, shape in (
        (main, factors_main, (ROWS, LANES)),
        (rest, factors_rest, (8, LANES)),
    ):
        low = jnp.zeros(shape, jnp.float32)
        back = jnp.zeros(shape, jnp.float32)
        for k in range(LEVELS):
            choose = load(offsets, k)
            high = load(coupling, k) if k < LEVELS - 1 else jnp.zeros(shape, jnp.float32)
            scale = 1.0 / (1.0 + low + high - low * back)
            back = high * scale
            factors[0, k] = jnp.where(choose == 0, -scale, scale)
            factors[1, k] = low * scale
            factors[2, k] = jnp.where(choose == 2, -back, back)
            low = high


def column_kernel(received, factors_main, factors_rest, send):
    lane = lane_ids(8)

    def main(k):
        base = (k % 2) * ROWS
        return [received[k // 2, base + 32 * f : base + 32 * f + ROWS, :] for f in range(4)]

    def rest(k):
        base = 128 + 8 * (k % 2)
        return received[k // 2, base : base + 8, :]

    def picked(below, above, sums):
        return jnp.where(below, sums[0], jnp.where(above, sums[2], sums[1]))

    solve_main = [jnp.zeros((ROWS, LANES), jnp.float32)] * 3
    solve_rest = jnp.zeros((8, LANES), jnp.float32)
    main_here, rest_here = main(0), rest(0)
    main_sums, rest_sums = [], []

    def push(k):
        nonlocal main_here, rest_here
        main_next, rest_next = main(k + 1), rest(k + 1)
        main_sums.append([a + b for a, b in zip(main_here, main_next)])
        rest_sums.append(rest_here + rest_next)
        main_here, rest_here = main_next, rest_next

    push(0)
    for k in range(LEVELS):
        if k + 1 < LEVELS - 1:
            push(k + 1)
        three = [max(k - 1, 0), min(k, LEVELS - 2), min(k + 1, LEVELS - 2)]
        scale = factors_main[0, k]
        below, above = scale < 0.0, factors_main[2, k] < 0.0
        values = [picked(below, above, [main_sums[i][f] for i in three]) for f in range(4)]
        weight = jnp.abs(scale) / values[3]
        low = factors_main[1, k]
        solve_main = [values[f] * weight + low * solve_main[f] for f in range(3)]
        for f in range(3):
            base = (f * 2 + k % 2) * ROWS
            send[k // 2, base : base + ROWS, :] = solve_main[f]
        scale = factors_rest[0, k]
        below, above = scale < 0.0, factors_rest[2, k] < 0.0
        value = picked(below, above, [rest_sums[i] for i in three])
        total = jnp.where(lane >= 64, pltpu.roll(value, 96, 1), pltpu.roll(value, 32, 1))
        total = jnp.where(lane >= 32, jnp.where(lane >= 64, total, pltpu.roll(value, 64, 1)), total)
        solve_rest = value * (jnp.abs(scale) / total) + factors_rest[1, k] * solve_rest
        base = 96 + 8 * (k % 2)
        send[k // 2, base : base + 8, :] = solve_rest
    for k in range(LEVELS - 2, -1, -1):
        back = jnp.abs(factors_main[2, k])
        for f in range(3):
            base = (f * 2 + k % 2) * ROWS
            solve_main[f] = send[k // 2, base : base + ROWS, :] + back * solve_main[f]
            send[k // 2, base : base + ROWS, :] = solve_main[f]
        base = 96 + 8 * (k % 2)
        solve_rest = send[k // 2, base : base + 8, :] + jnp.abs(factors_rest[2, k]) * solve_rest
        send[k // 2, base : base + 8, :] = solve_rest


def unpack_kernel(received, tracer_out, u_out, v_out, whole, sems):
    lane = lane_ids(ROWS)
    copies = []
    for field, out in enumerate((tracer_out, u_out, v_out)):
        for level in range(2):
            base = (field * 2 + level) * ROWS
            for tile in range(LON // LANES):
                source = tile if tile < 8 else tile - 1
                fresh = tile != 8 and tile != 17
                shift = 16 * (source % 8) if fresh else LANES
                value = received[source, base : base + ROWS, :] if fresh else None
                if shift > 0:
                    last = source - 1 if fresh else (7 if tile == 8 else 15)
                    place = shift - 16
                    packed = received[last, 96 + 8 * level : 104 + 8 * level, :]
                    start = place - 32 * field
                    rest = jnp.concatenate(
                        [
                            pltpu.roll(packed, start % LANES, 1),
                            pltpu.roll(pltpu.roll(packed, 6, 0), (start - 16) % LANES, 1),
                        ],
                        axis=0,
                    )
                    old = received[last, base : base + ROWS, :]
                    old = jnp.where(lane >= place, rest, old) if place > 0 else rest
                    value = jnp.where(lane >= shift, value, old) if fresh else old
                whole[field, level, :, tile * LANES : (tile + 1) * LANES] = value
            copy = pltpu.make_async_copy(
                whole.at[field, level], out.at[level], sems.at[2 * field + level]
            )
            copy.start()
            copies.append(copy)
    for copy in copies:
        copy.wait()


def call(kernel, in_specs, outs, scratch=(), aliases=None, flops=1000000, nbytes=3000000):
    return pl.pallas_call(
        kernel,
        in_specs=in_specs,
        out_specs=[spec for spec, _ in outs],
        out_shape=[jax.ShapeDtypeStruct(shape, jnp.float32) for _, shape in outs],
        scratch_shapes=scratch,
        input_output_aliases=aliases or {},
        compiler_params=PARAMS,
        cost_estimate=pl.CostEstimate(flops=flops, bytes_accessed=nbytes, transcendentals=0),
    )


def local(tracer, thickness, wind_u, wind_v, offsets, coupling):
    f32 = jnp.float32
    lat_count = lax.axis_size("lat")
    slab = (2, ROWS, LON)
    halo = (5, 2, LON)
    chunks = (DEST, 144, LANES)
    winds = (tracer, thickness, wind_u, wind_v)
    to_first, to_second, kept = call(
        edge_kernel,
        [HB] * 4,
        [(VM, halo), (VM, halo), (VM, (8, 8, LON))],
        scratch=[pltpu.VMEM((4, 8, LON), f32), pltpu.SemaphoreType.DMA((16,))],
    )(*[pltpu.with_memory_space_constraint(x, pltpu.HBM) for x in winds])
    pairs = [[(i, i + 1) for i in range(start, lat_count - 1, 2)] for start in (1, 0)]
    first_halo, second_halo = [
        lax.ppermute(rows, "lat", [p for a, b in pair for p in ((a, b), (b, a))])
        for rows, pair in zip((to_first, to_second), pairs)
    ]
    send, edges = call(
        first_kernel,
        [VM] * 4,
        [(ANY, chunks), (VM, (2, 8, LON))],
        scratch=[
            pltpu.VMEM((4,) + slab, f32),
            pltpu.VMEM(chunks, f32),
            pltpu.SemaphoreType.DMA((DEST,)),
        ],
    )(*winds)
    (send,) = call(
        second_kernel,
        [VM] * 4 + [ANY],
        [(ANY, chunks)],
        scratch=[
            pltpu.VMEM((4, 8, LON), f32),
            pltpu.VMEM(chunks, f32),
            pltpu.SemaphoreType.DMA((18,)),
        ],
        aliases={4: 0},
    )(first_halo, second_halo, kept, edges, send)
    received = lax.all_to_all(send, "lev", split_axis=0, concat_axis=0, tiled=True)
    factors = call(
        factor_kernel,
        [VM, VM],
        [(VM, (3, LEVELS, ROWS, LANES)), (VM, (3, LEVELS, 8, LANES))],
    )(offsets, coupling)
    (back,) = call(column_kernel, [VM] * 3, [(VM, (DEST, 112, LANES))])(received, *factors)
    returned = lax.all_to_all(back, "lev", split_axis=0, concat_axis=0, tiled=True)
    return tuple(
        call(
            unpack_kernel,
            [VM],
            [(ANY, slab)] * 3,
            scratch=[pltpu.VMEM((3,) + slab, f32), pltpu.SemaphoreType.DMA((6,))],
        )(returned)
    )


def solution(mesh):
    return jax.shard_map(
        local,
        mesh=mesh,
        in_specs=(
            P("lev", "lat", None),
            P("lev", "lat", None),
            P("lev", "lat", None),
            P("lev", "lat", None),
            P(None, "lat", "lev"),
            P(None, "lat", "lev"),
        ),
        out_specs=(P("lev", "lat", None), P("lev", "lat", None), P("lev", "lat", None)),
        check_vma=False,
    )
```

```python
import jax
import jax.numpy as jnp
from jax import lax
from jax.experimental import pallas as pl
from jax.experimental.pallas import tpu as pltpu
from jax.sharding import PartitionSpec as P

courant_max = 0.24
LEVELS = 32
LON = 2304
ROWS = 16
DEST = 16
COLS = 144
LANES = 128
VM = pl.BlockSpec(memory_space=pltpu.VMEM)
ANY = pl.BlockSpec(memory_space=pl.ANY)
HB = pl.BlockSpec(memory_space=pltpu.HBM)
PARAMS = pltpu.CompilerParams(vmem_limit_bytes=24 * 1024 * 1024)


def lane_ids(rows):
    return lax.broadcasted_iota(jnp.int32, (rows, LANES), 1)


def row_ids(rows):
    return lax.broadcasted_iota(jnp.int32, (rows, LON), 0)


def courant(pair_sum):
    return courant_max * jnp.tanh(0.5 * pair_sum)


def upwind(flow, before, after):
    return jnp.maximum(flow, 0.0) * before + jnp.minimum(flow, 0.0) * after


def east_roll(x):
    return pltpu.roll(x, 1, 1)


def west_roll(x):
    return pltpu.roll(x, LON - 1, 1)


def zonal(east, mass):
    flux = upwind(east, east_roll(mass), mass)
    return flux - west_roll(flux)


def edge_kernel(tracer, thickness, wind_u, wind_v, to_first, to_second, kept, fetched, sems):
    copies = [
        pltpu.make_async_copy(
            ref.at[:, pl.ds(14 * end, 2), :],
            fetched.at[slot, :, pl.ds(2 * end, 2), :],
            sems.at[2 * slot + end],
        )
        for slot, ref in enumerate((tracer, thickness, wind_u, wind_v))
        for end in range(2)
    ]
    for copy in copies:
        copy.start()
    for copy in copies:
        copy.wait()
    tracer, layer, u, v = [
        jnp.concatenate([fetched[slot, 0], fetched[slot, 1]], axis=0) for slot in range(4)
    ]
    mass = tracer * layer
    east = courant(east_roll(u) + u)
    north = courant(v + pltpu.roll(v, 7, 0))
    odd = lax.rem(row_ids(8), 2) == 1
    upper = lax.rem(row_ids(8), 4) >= 2
    inner = jnp.where(odd, pltpu.roll(north, 1, 0), north)

    def partial(m):
        flux = upwind(north, m, pltpu.roll(m, 7, 0))
        return m + zonal(east, m) + jnp.where(odd, pltpu.roll(flux, 1, 0), -flux)

    values = (v, mass, layer, partial(mass), partial(layer))
    odd_lat = lax.rem(lax.axis_index("lat"), 2) == 1
    north_first = jnp.broadcast_to(odd_lat, (1, LON))
    for slot, value in enumerate(values):
        for level in range(2):
            south = value[4 * level : 4 * level + 1]
            north_row = value[4 * level + 3 : 4 * level + 4]
            to_first[slot, level : level + 1, :] = jnp.where(north_first, north_row, south)
            to_second[slot, level : level + 1, :] = jnp.where(north_first, south, north_row)
        kept[slot] = value
    kept[5] = east
    kept[6] = jnp.where(upper, jnp.minimum(inner, 0.0), -jnp.maximum(inner, 0.0))


def pack_pair(load, store, places):
    lane = lane_ids(ROWS)
    lane8 = lane_ids(8)
    for dest in range(DEST):
        tile = dest + dest // 8
        shift = 16 * (dest % 8)
        packed = None
        for place, field, level in places:
            here, after = load(field, level, tile), load(field, level, tile + 1)
            block = here if shift == 0 else jnp.where(lane >= shift, here, after)
            store(dest, (field * 2 + level) * ROWS, block)
            for half in range(2):
                part = after[8 * half : 8 * half + 8]
                part = pltpu.roll(part, 2, 0) if half else part
                start = place + 16 * half
                part = pltpu.roll(part, (start - shift) % LANES, 1)
                packed = part if packed is None else jnp.where(lane8 >= start, part, packed)
        store(dest, 64, packed)


def first_kernel(tracer, thickness, wind_u, wind_v, send, edges, held):
    row = row_ids(ROWS)
    for level in range(2):
        u, v, layer = wind_u[level], wind_v[level], thickness[level]
        mass = tracer[level] * layer
        east = courant(east_roll(u) + u)
        north = jnp.where(row == 0, 0.0, courant(pltpu.roll(v, 1, 0) + v))
        for slot, m in enumerate((mass, layer)):
            for substep in range(2):
                flux = upwind(north, pltpu.roll(m, 1, 0), m)
                above = jnp.where(row == ROWS - 1, 0.0, pltpu.roll(flux, ROWS - 1, 0))
                m = m + zonal(east, m) + flux - above
            edges[slot, 4 * level : 4 * level + 2, :] = m[0:2]
            edges[slot, 4 * level + 2 : 4 * level + 4, :] = m[14:16]
            held[slot, level] = m

    def load(field, level, tile):
        return held[field, level, :, tile * LANES : (tile + 1) * LANES]

    def load_wind(field, level, tile):
        return (wind_u, wind_v)[field][level, :, tile * LANES : (tile + 1) * LANES]

    def store(dest, row, value):
        send[dest, row : row + value.shape[0], :] = value

    def store_wind(dest, row, value):
        store(dest, 72 + row, value)

    pack_pair(load, store, ((0, 0, 0), (32, 1, 0), (64, 0, 1), (96, 1, 1)))
    pack_pair(load_wind, store_wind, ((0, 1, 1), (32, 0, 0), (64, 1, 0), (96, 0, 1)))


def second_kernel(first_halo, second_halo, kept, edges, sent, send, held, patch, sems):
    lat = lax.axis_index("lat")
    row = lax.rem(row_ids(8), 4)
    upper = row >= 2
    outer = (row == 0) | (row == 3)
    even = jnp.broadcast_to(lax.rem(lat, 2) == 0, (1, LON))
    south_open = jnp.where(lat > 0, 1.0, 0.0)
    north_open = jnp.where(lat < lax.axis_size("lat") - 1, 1.0, 0.0)
    open_face = jnp.where(upper, north_open, south_open)

    def halo(slot):
        rows = []
        for level in range(2):
            one = first_halo[slot, level : level + 1, :]
            two = second_halo[slot, level : level + 1, :]
            south = jnp.where(even, one, two)
            north = jnp.where(even, two, one)
            rows.append(jnp.where(upper[0:4], north, south))
        return jnp.concatenate(rows, axis=0)

    v, east, inner = kept[0], kept[5], kept[6]
    flow = open_face * courant(v + halo(0))
    sign = jnp.where(upper, -1.0, 1.0)
    for slot in range(2):
        m, m_beyond = kept[1 + slot], halo(1 + slot)
        partial, beyond = kept[3 + slot], halo(3 + slot)
        flux = upwind(flow, jnp.where(upper, m, m_beyond), jnp.where(upper, m_beyond, m))
        change = jnp.where(outer, sign * flux, 0.0)
        partial = partial + change
        beyond = beyond - change
        flux = upwind(flow, jnp.where(upper, partial, beyond), jnp.where(upper, beyond, partial))
        carried = inner * change
        gain = change + zonal(east, change) + carried + sign * flux
        passed = jnp.where(row == 1, pltpu.roll(carried, 1, 0), pltpu.roll(carried, 7, 0))
        held[slot] = edges[slot] + jnp.where(outer, gain, -passed)
    lane = lane_ids(8)
    for dest in range(DEST):
        tile = dest + dest // 8
        shift = 16 * (dest % 8)
        low = slice(tile * LANES, (tile + 1) * LANES)
        high = slice((tile + 1) * LANES, (tile + 2) * LANES)
        packed = None
        for level in range(2):
            for field in range(2):
                here, after = held[field, :, low], held[field, :, high]
                block = here if shift == 0 else jnp.where(lane >= shift, here, after)
                start = (field * 2 + level) * ROWS
                patch[dest, start : start + 2, :] = block[4 * level : 4 * level + 2]
                patch[dest, start + 14 : start + 16, :] = block[4 * level + 2 : 4 * level + 4]
                for half in range(2):
                    start = 64 * level + 32 * field + 16 * half
                    part = pltpu.roll(after, (8 - 4 * level - 2 * half) % 8, 0)
                    part = pltpu.roll(part, (start - shift) % LANES, 1)
                    packed = part if packed is None else jnp.where(lane >= start, part, packed)
        patch[dest, 64:66, :] = packed[0:2]
    spots = [16 * i + end for i in range(4) for end in (0, 14)] + [64]
    copies = [
        pltpu.make_async_copy(
            patch.at[:, pl.ds(spot, 2), :], send.at[:, pl.ds(spot, 2), :], sems.at[i]
        )
        for i, spot in enumerate(spots)
    ]
    for copy in copies:
        copy.start()
    for copy in copies:
        copy.wait()


def factor_kernel(offsets, coupling, factors_main, factors_rest):
    shift = 16 * lax.rem(lax.axis_index("lev"), 8)
    half = lax.rem(lane_ids(8), 32) >= 16

    def main(ref, k):
        return pltpu.roll(ref[k, :, 0:LANES], shift, 1)

    def rest(ref, k):
        part = ref[k, :, LANES:COLS]
        both = jnp.concatenate([part[0:8], part[8:16]], axis=1)
        all_fields = jnp.concatenate([both, both, both, both], axis=1)
        return jnp.where(half, pltpu.roll(all_fields, 2, 0), all_fields)

    for load, factors, shape in (
        (main, factors_main, (ROWS, LANES)),
        (rest, factors_rest, (8, LANES)),
    ):
        low = jnp.zeros(shape, jnp.float32)
        back = jnp.zeros(shape, jnp.float32)
        for k in range(LEVELS):
            choose = load(offsets, k)
            high = load(coupling, k) if k < LEVELS - 1 else jnp.zeros(shape, jnp.float32)
            scale = 1.0 / (1.0 + low + high - low * back)
            back = high * scale
            factors[0, k] = jnp.where(choose == 0, -scale, scale)
            factors[1, k] = low * scale
            factors[2, k] = jnp.where(choose == 2, -back, back)
            low = high


def column_kernel(received, factors_main, factors_rest, send):
    group = lane_ids(8) // 32

    def main(k):
        base = (k % 2) * ROWS
        mass, layer = [received[k // 2, base + 32 * f : base + 32 * f + ROWS, :] for f in range(2)]
        u, v = [received[k // 2, base + 72 + 32 * f : base + 72 + 32 * f + ROWS, :] for f in range(2)]
        return [mass, layer * u, layer * v, layer]

    def rest(k):
        mass, wind = received[k // 2, 64:72, :], received[k // 2, 136:144, :]
        if k % 2:
            mass, wind = pltpu.roll(mass, 64, 1), pltpu.roll(wind, 64, 1)
        layer = jnp.where(group == 0, pltpu.roll(mass, 96, 1), mass)
        layer = jnp.where(group >= 2, pltpu.roll(layer, 64, 1), layer)
        return [jnp.where(group == 0, mass, layer * wind), layer]

    def picked(below, above, sums):
        return jnp.where(below, sums[0], jnp.where(above, sums[2], sums[1]))

    solve_main = [jnp.zeros((ROWS, LANES), jnp.float32)] * 3
    solve_rest = jnp.zeros((8, LANES), jnp.float32)
    main_here, rest_here = main(0), rest(0)
    main_sums, rest_sums = [], []

    def push(k):
        nonlocal main_here, rest_here
        main_next, rest_next = main(k + 1), rest(k + 1)
        main_sums.append([a + b for a, b in zip(main_here, main_next)])
        rest_sums.append([a + b for a, b in zip(rest_here, rest_next)])
        main_here, rest_here = main_next, rest_next

    push(0)
    for k in range(LEVELS):
        if k + 1 < LEVELS - 1:
            push(k + 1)
        three = [max(k - 1, 0), min(k, LEVELS - 2), min(k + 1, LEVELS - 2)]
        scale = factors_main[0, k]
        below, above = scale < 0.0, factors_main[2, k] < 0.0
        values = [picked(below, above, [main_sums[i][f] for i in three]) for f in range(4)]
        weight = jnp.abs(scale) / values[3]
        low = factors_main[1, k]
        solve_main = [values[f] * weight + low * solve_main[f] for f in range(3)]
        for f in range(3):
            base = (f * 2 + k % 2) * ROWS
            send[k // 2, base : base + ROWS, :] = solve_main[f]
        scale = factors_rest[0, k]
        below, above = scale < 0.0, factors_rest[2, k] < 0.0
        value, total = [picked(below, above, [rest_sums[i][f] for i in three]) for f in range(2)]
        solve_rest = value * (jnp.abs(scale) / total) + factors_rest[1, k] * solve_rest
        base = 96 + 8 * (k % 2)
        send[k // 2, base : base + 8, :] = solve_rest
    for k in range(LEVELS - 2, -1, -1):
        back = jnp.abs(factors_main[2, k])
        for f in range(3):
            base = (f * 2 + k % 2) * ROWS
            solve_main[f] = send[k // 2, base : base + ROWS, :] + back * solve_main[f]
            send[k // 2, base : base + ROWS, :] = solve_main[f]
        base = 96 + 8 * (k % 2)
        solve_rest = send[k // 2, base : base + 8, :] + jnp.abs(factors_rest[2, k]) * solve_rest
        send[k // 2, base : base + 8, :] = solve_rest


def unpack_kernel(received, tracer_out, u_out, v_out, whole, sems):
    lane = lane_ids(ROWS)
    copies = []
    for field, out in enumerate((tracer_out, u_out, v_out)):
        for level in range(2):
            base = (field * 2 + level) * ROWS
            for tile in range(LON // LANES):
                source = tile if tile < 8 else tile - 1
                fresh = tile != 8 and tile != 17
                shift = 16 * (source % 8) if fresh else LANES
                value = received[source, base : base + ROWS, :] if fresh else None
                if shift > 0:
                    last = source - 1 if fresh else (7 if tile == 8 else 15)
                    place = shift - 16
                    packed = received[last, 96 + 8 * level : 104 + 8 * level, :]
                    start = place - 32 * field
                    rest = jnp.concatenate(
                        [
                            pltpu.roll(packed, start % LANES, 1),
                            pltpu.roll(pltpu.roll(packed, 6, 0), (start - 16) % LANES, 1),
                        ],
                        axis=0,
                    )
                    old = received[last, base : base + ROWS, :]
                    old = jnp.where(lane >= place, rest, old) if place > 0 else rest
                    value = jnp.where(lane >= shift, value, old) if fresh else old
                whole[field, level, :, tile * LANES : (tile + 1) * LANES] = value
            copy = pltpu.make_async_copy(
                whole.at[field, level], out.at[level], sems.at[2 * field + level]
            )
            copy.start()
            copies.append(copy)
    for copy in copies:
        copy.wait()


def call(kernel, in_specs, outs, scratch=(), aliases=None, flops=1000000, nbytes=3000000):
    return pl.pallas_call(
        kernel,
        in_specs=in_specs,
        out_specs=[spec for spec, _ in outs],
        out_shape=[jax.ShapeDtypeStruct(shape, jnp.float32) for _, shape in outs],
        scratch_shapes=scratch,
        input_output_aliases=aliases or {},
        compiler_params=PARAMS,
        cost_estimate=pl.CostEstimate(flops=flops, bytes_accessed=nbytes, transcendentals=0),
    )


def local(tracer, thickness, wind_u, wind_v, offsets, coupling):
    f32 = jnp.float32
    lat_count = lax.axis_size("lat")
    slab = (2, ROWS, LON)
    halo = (5, 2, LON)
    chunks = (DEST, 144, LANES)

    def transposed(block):
        return lax.all_to_all(block, "lev", split_axis=0, concat_axis=0, tiled=True)

    fields = [
        pltpu.with_memory_space_constraint(x, pltpu.HBM)
        for x in (tracer, thickness, wind_u, wind_v)
    ]
    to_first, to_second, kept = call(
        edge_kernel,
        [HB] * 4,
        [(VM, halo), (VM, halo), (VM, (7, 8, LON))],
        scratch=[pltpu.VMEM((4, 2, 4, LON), f32), pltpu.SemaphoreType.DMA((8,))],
    )(*fields)
    pairs = [[(i, i + 1) for i in range(start, lat_count - 1, 2)] for start in (1, 0)]
    first_halo, second_halo = [
        lax.ppermute(rows, "lat", [p for a, b in pair for p in ((a, b), (b, a))])
        for rows, pair in zip((to_first, to_second), pairs)
    ]
    send, edges = call(
        first_kernel,
        [VM] * 4,
        [(VM, chunks), (VM, (2, 8, LON))],
        scratch=[pltpu.VMEM((2,) + slab, f32)],
    )(tracer, thickness, wind_u, wind_v)
    factors = call(
        factor_kernel,
        [VM, VM],
        [(VM, (3, LEVELS, ROWS, LANES)), (VM, (3, LEVELS, 8, LANES))],
    )(offsets, coupling)
    edges, *factors = lax.optimization_barrier((edges, *factors))
    (send,) = call(
        second_kernel,
        [VM] * 4 + [ANY],
        [(ANY, chunks)],
        scratch=[
            pltpu.VMEM((2, 8, LON), f32),
            pltpu.VMEM((DEST, 72, LANES), f32),
            pltpu.SemaphoreType.DMA((9,)),
        ],
        aliases={4: 0},
    )(first_halo, second_halo, kept, edges, send)
    received = transposed(send)
    (back,) = call(column_kernel, [VM] * 3, [(VM, (DEST, 112, LANES))])(received, *factors)
    returned = transposed(back)
    return tuple(
        call(
            unpack_kernel,
            [VM],
            [(ANY, slab)] * 3,
            scratch=[pltpu.VMEM((3,) + slab, f32), pltpu.SemaphoreType.DMA((6,))],
        )(returned)
    )


def solution(mesh):
    return jax.shard_map(
        local,
        mesh=mesh,
        in_specs=(
            P("lev", "lat", None),
            P("lev", "lat", None),
            P("lev", "lat", None),
            P("lev", "lat", None),
            P(None, "lat", "lev"),
            P(None, "lat", "lev"),
        ),
        out_specs=(P("lev", "lat", None), P("lev", "lat", None), P("lev", "lat", None)),
        check_vma=False,
    )
```

```python
import jax
import jax.numpy as jnp
from jax import lax
from jax.experimental import pallas as pl
from jax.experimental.pallas import tpu as pltpu
from jax.sharding import PartitionSpec as P

courant_max = 0.24
LEVELS = 32
LON = 2304
ROWS = 16
DEST = 16
COLS = 144
LANES = 128
VM = pl.BlockSpec(memory_space=pltpu.VMEM)
ANY = pl.BlockSpec(memory_space=pl.ANY)
HB = pl.BlockSpec(memory_space=pltpu.HBM)
PARAMS = pltpu.CompilerParams(vmem_limit_bytes=24 * 1024 * 1024)


def lane_ids(rows):
    return lax.broadcasted_iota(jnp.int32, (rows, LANES), 1)


def row_ids(rows):
    return lax.broadcasted_iota(jnp.int32, (rows, LON), 0)


def courant(pair_sum):
    return courant_max * jnp.tanh(0.5 * pair_sum)


def upwind(flow, before, after):
    return jnp.maximum(flow, 0.0) * before + jnp.minimum(flow, 0.0) * after


def east_roll(x):
    return pltpu.roll(x, 1, 1)


def west_roll(x):
    return pltpu.roll(x, LON - 1, 1)


def zonal(east, mass):
    flux = upwind(east, east_roll(mass), mass)
    return flux - west_roll(flux)


def edge_kernel(tracer, thickness, wind_u, wind_v, to_first, to_second, kept, fetched, sems):
    copies = [
        pltpu.make_async_copy(
            ref.at[:, pl.ds(14 * end, 2), :],
            fetched.at[slot, :, pl.ds(2 * end, 2), :],
            sems.at[2 * slot + end],
        )
        for slot, ref in enumerate((tracer, thickness, wind_u, wind_v))
        for end in range(2)
    ]
    for copy in copies:
        copy.start()
    for copy in copies:
        copy.wait()
    tracer, layer, u, v = [
        jnp.concatenate([fetched[slot, 0], fetched[slot, 1]], axis=0) for slot in range(4)
    ]
    mass = tracer * layer
    east = courant(east_roll(u) + u)
    north = courant(v + pltpu.roll(v, 7, 0))
    odd = lax.rem(row_ids(8), 2) == 1
    upper = lax.rem(row_ids(8), 4) >= 2
    inner = jnp.where(odd, pltpu.roll(north, 1, 0), north)

    def partial(m):
        flux = upwind(north, m, pltpu.roll(m, 7, 0))
        return m + zonal(east, m) + jnp.where(odd, pltpu.roll(flux, 1, 0), -flux)

    values = (v, mass, layer, partial(mass), partial(layer))
    odd_lat = lax.rem(lax.axis_index("lat"), 2) == 1
    north_first = jnp.broadcast_to(odd_lat, (1, LON))
    for slot, value in enumerate(values):
        for level in range(2):
            south = value[4 * level : 4 * level + 1]
            north_row = value[4 * level + 3 : 4 * level + 4]
            to_first[slot, level : level + 1, :] = jnp.where(north_first, north_row, south)
            to_second[slot, level : level + 1, :] = jnp.where(north_first, south, north_row)
        kept[slot] = value
    kept[5] = east
    kept[6] = jnp.where(upper, jnp.minimum(inner, 0.0), -jnp.maximum(inner, 0.0))


def pack_pair(load, store, places):
    lane = lane_ids(ROWS)
    lane8 = lane_ids(8)
    for dest in range(DEST):
        tile = dest + dest // 8
        shift = 16 * (dest % 8)
        packed = None
        for place, field, level in places:
            here, after = load(field, level, tile), load(field, level, tile + 1)
            block = here if shift == 0 else jnp.where(lane >= shift, here, after)
            store(dest, (field * 2 + level) * ROWS, block)
            for half in range(2):
                part = after[8 * half : 8 * half + 8]
                part = pltpu.roll(part, 2, 0) if half else part
                start = place + 16 * half
                part = pltpu.roll(part, (start - shift) % LANES, 1)
                packed = part if packed is None else jnp.where(lane8 >= start, part, packed)
        store(dest, 64, packed)


def first_kernel(tracer, thickness, wind_u, wind_v, send, edges, held):
    row = row_ids(ROWS)
    for level in range(2):
        u, v, layer = wind_u[level], wind_v[level], thickness[level]
        mass = tracer[level] * layer
        east = courant(east_roll(u) + u)
        north = jnp.where(row == 0, 0.0, courant(pltpu.roll(v, 1, 0) + v))
        for slot, m in enumerate((mass, layer)):
            for substep in range(2):
                flux = upwind(north, pltpu.roll(m, 1, 0), m)
                above = jnp.where(row == ROWS - 1, 0.0, pltpu.roll(flux, ROWS - 1, 0))
                m = m + zonal(east, m) + flux - above
            edges[slot, 4 * level : 4 * level + 2, :] = m[0:2]
            edges[slot, 4 * level + 2 : 4 * level + 4, :] = m[14:16]
            held[slot, level] = m

    def load(field, level, tile):
        return held[field, level, :, tile * LANES : (tile + 1) * LANES]

    def load_wind(field, level, tile):
        return (wind_u, wind_v)[field][level, :, tile * LANES : (tile + 1) * LANES]

    def store(dest, row, value):
        send[dest, row : row + value.shape[0], :] = value

    def store_wind(dest, row, value):
        store(dest, 72 + row, value)

    pack_pair(load, store, ((0, 0, 0), (32, 1, 0), (64, 0, 1), (96, 1, 1)))
    pack_pair(load_wind, store_wind, ((0, 1, 1), (32, 0, 0), (64, 1, 0), (96, 0, 1)))


def second_kernel(first_halo, second_halo, kept, edges, sent, send, held, patch, sems):
    lat = lax.axis_index("lat")
    row = lax.rem(row_ids(8), 4)
    upper = row >= 2
    outer = (row == 0) | (row == 3)
    even = jnp.broadcast_to(lax.rem(lat, 2) == 0, (1, LON))
    south_open = jnp.where(lat > 0, 1.0, 0.0)
    north_open = jnp.where(lat < lax.axis_size("lat") - 1, 1.0, 0.0)
    open_face = jnp.where(upper, north_open, south_open)

    def halo(slot):
        rows = []
        for level in range(2):
            one = first_halo[slot, level : level + 1, :]
            two = second_halo[slot, level : level + 1, :]
            south = jnp.where(even, one, two)
            north = jnp.where(even, two, one)
            rows.append(jnp.where(upper[0:4], north, south))
        return jnp.concatenate(rows, axis=0)

    v, east, inner = kept[0], kept[5], kept[6]
    flow = open_face * courant(v + halo(0))
    sign = jnp.where(upper, -1.0, 1.0)
    for slot in range(2):
        m, m_beyond = kept[1 + slot], halo(1 + slot)
        partial, beyond = kept[3 + slot], halo(3 + slot)
        flux = upwind(flow, jnp.where(upper, m, m_beyond), jnp.where(upper, m_beyond, m))
        change = jnp.where(outer, sign * flux, 0.0)
        partial = partial + change
        beyond = beyond - change
        flux = upwind(flow, jnp.where(upper, partial, beyond), jnp.where(upper, beyond, partial))
        carried = inner * change
        gain = change + zonal(east, change) + carried + sign * flux
        passed = jnp.where(row == 1, pltpu.roll(carried, 1, 0), pltpu.roll(carried, 7, 0))
        held[slot] = edges[slot] + jnp.where(outer, gain, -passed)
    lane = lane_ids(8)
    for dest in range(DEST):
        tile = dest + dest // 8
        shift = 16 * (dest % 8)
        low = slice(tile * LANES, (tile + 1) * LANES)
        high = slice((tile + 1) * LANES, (tile + 2) * LANES)
        packed = None
        for level in range(2):
            for field in range(2):
                here, after = held[field, :, low], held[field, :, high]
                block = here if shift == 0 else jnp.where(lane >= shift, here, after)
                start = (field * 2 + level) * ROWS
                patch[dest, start : start + 2, :] = block[4 * level : 4 * level + 2]
                patch[dest, start + 14 : start + 16, :] = block[4 * level + 2 : 4 * level + 4]
                for half in range(2):
                    start = 64 * level + 32 * field + 16 * half
                    part = pltpu.roll(after, (8 - 4 * level - 2 * half) % 8, 0)
                    part = pltpu.roll(part, (start - shift) % LANES, 1)
                    packed = part if packed is None else jnp.where(lane >= start, part, packed)
        patch[dest, 64:66, :] = packed[0:2]
    spots = [16 * i + end for i in range(4) for end in (0, 14)] + [64]
    copies = [
        pltpu.make_async_copy(
            patch.at[:, pl.ds(spot, 2), :], send.at[:, pl.ds(spot, 2), :], sems.at[i]
        )
        for i, spot in enumerate(spots)
    ]
    for copy in copies:
        copy.start()
    for copy in copies:
        copy.wait()


def factor_kernel(offsets, coupling, factors_main, factors_rest):
    shift = 16 * lax.rem(lax.axis_index("lev"), 8)
    half = lax.rem(lane_ids(8), 32) >= 16

    def main(ref, k):
        return pltpu.roll(ref[k, :, 0:LANES], shift, 1)

    def rest(ref, k):
        part = ref[k, :, LANES:COLS]
        both = jnp.concatenate([part[0:8], part[8:16]], axis=1)
        all_fields = jnp.concatenate([both, both, both, both], axis=1)
        return jnp.where(half, pltpu.roll(all_fields, 2, 0), all_fields)

    for load, factors, shape in (
        (main, factors_main, (ROWS, LANES)),
        (rest, factors_rest, (8, LANES)),
    ):
        low = jnp.zeros(shape, jnp.float32)
        back = jnp.zeros(shape, jnp.float32)
        for k in range(LEVELS):
            choose = load(offsets, k)
            high = load(coupling, k) if k < LEVELS - 1 else jnp.zeros(shape, jnp.float32)
            scale = 1.0 / (1.0 + low + high - low * back)
            back = high * scale
            factors[0, k] = jnp.where(choose == 0, -scale, scale)
            factors[1, k] = low * scale
            factors[2, k] = jnp.where(choose == 2, -back, back)
            low = high


def column_kernel(received, factors_main, factors_rest, send):
    group = lane_ids(8) // 32

    def main(k):
        base = (k % 2) * ROWS
        mass, layer = [received[k // 2, base + 32 * f : base + 32 * f + ROWS, :] for f in range(2)]
        u, v = [received[k // 2, base + 72 + 32 * f : base + 72 + 32 * f + ROWS, :] for f in range(2)]
        return [mass, layer * u, layer * v, layer]

    def rest(k):
        mass, wind = received[k // 2, 64:72, :], received[k // 2, 136:144, :]
        if k % 2:
            mass, wind = pltpu.roll(mass, 64, 1), pltpu.roll(wind, 64, 1)
        layer = jnp.where(group == 0, pltpu.roll(mass, 96, 1), mass)
        layer = jnp.where(group >= 2, pltpu.roll(layer, 64, 1), layer)
        return [jnp.where(group == 0, mass, layer * wind), layer]

    def picked(below, above, sums):
        return jnp.where(below, sums[0], jnp.where(above, sums[2], sums[1]))

    solve_main = [jnp.zeros((ROWS, LANES), jnp.float32)] * 3
    solve_rest = jnp.zeros((8, LANES), jnp.float32)
    main_here, rest_here = main(0), rest(0)
    main_sums, rest_sums = [], []

    def push(k):
        nonlocal main_here, rest_here
        main_next, rest_next = main(k + 1), rest(k + 1)
        main_sums.append([a + b for a, b in zip(main_here, main_next)])
        rest_sums.append([a + b for a, b in zip(rest_here, rest_next)])
        main_here, rest_here = main_next, rest_next

    push(0)
    for k in range(LEVELS):
        if k + 1 < LEVELS - 1:
            push(k + 1)
        three = [max(k - 1, 0), min(k, LEVELS - 2), min(k + 1, LEVELS - 2)]
        scale = factors_main[0, k]
        below, above = scale < 0.0, factors_main[2, k] < 0.0
        values = [picked(below, above, [main_sums[i][f] for i in three]) for f in range(4)]
        weight = jnp.abs(scale) / values[3]
        low = factors_main[1, k]
        solve_main = [values[f] * weight + low * solve_main[f] for f in range(3)]
        for f in range(3):
            base = (f * 2 + k % 2) * ROWS
            send[k // 2, base : base + ROWS, :] = solve_main[f]
        scale = factors_rest[0, k]
        below, above = scale < 0.0, factors_rest[2, k] < 0.0
        value, total = [picked(below, above, [rest_sums[i][f] for i in three]) for f in range(2)]
        solve_rest = value * (jnp.abs(scale) / total) + factors_rest[1, k] * solve_rest
        base = 96 + 8 * (k % 2)
        send[k // 2, base : base + 8, :] = solve_rest
    for k in range(LEVELS - 2, -1, -1):
        back = jnp.abs(factors_main[2, k])
        for f in range(3):
            base = (f * 2 + k % 2) * ROWS
            solve_main[f] = send[k // 2, base : base + ROWS, :] + back * solve_main[f]
            send[k // 2, base : base + ROWS, :] = solve_main[f]
        base = 96 + 8 * (k % 2)
        solve_rest = send[k // 2, base : base + 8, :] + jnp.abs(factors_rest[2, k]) * solve_rest
        send[k // 2, base : base + 8, :] = solve_rest


def unpack_kernel(received, tracer_out, u_out, v_out, whole, sems):
    lane = lane_ids(ROWS)
    copies = []
    for field, out in enumerate((tracer_out, u_out, v_out)):
        for level in range(2):
            base = (field * 2 + level) * ROWS
            for tile in range(LON // LANES):
                source = tile if tile < 8 else tile - 1
                fresh = tile != 8 and tile != 17
                shift = 16 * (source % 8) if fresh else LANES
                value = received[source, base : base + ROWS, :] if fresh else None
                if shift > 0:
                    last = source - 1 if fresh else (7 if tile == 8 else 15)
                    place = shift - 16
                    packed = received[last, 96 + 8 * level : 104 + 8 * level, :]
                    start = place - 32 * field
                    rest = jnp.concatenate(
                        [
                            pltpu.roll(packed, start % LANES, 1),
                            pltpu.roll(pltpu.roll(packed, 6, 0), (start - 16) % LANES, 1),
                        ],
                        axis=0,
                    )
                    old = received[last, base : base + ROWS, :]
                    old = jnp.where(lane >= place, rest, old) if place > 0 else rest
                    value = jnp.where(lane >= shift, value, old) if fresh else old
                whole[field, level, :, tile * LANES : (tile + 1) * LANES] = value
            copy = pltpu.make_async_copy(
                whole.at[field, level], out.at[level], sems.at[2 * field + level]
            )
            copy.start()
            copies.append(copy)
    for copy in copies:
        copy.wait()


def call(kernel, in_specs, outs, scratch=(), aliases=None, flops=1000000, nbytes=3000000):
    return pl.pallas_call(
        kernel,
        in_specs=in_specs,
        out_specs=[spec for spec, _ in outs],
        out_shape=[jax.ShapeDtypeStruct(shape, jnp.float32) for _, shape in outs],
        scratch_shapes=scratch,
        input_output_aliases=aliases or {},
        compiler_params=PARAMS,
        cost_estimate=pl.CostEstimate(flops=flops, bytes_accessed=nbytes, transcendentals=0),
    )


def local(tracer, thickness, wind_u, wind_v, offsets, coupling):
    f32 = jnp.float32
    lat_count = lax.axis_size("lat")
    slab = (2, ROWS, LON)
    halo = (5, 2, LON)
    chunks = (DEST, 144, LANES)

    def transposed(block):
        return lax.all_to_all(block, "lev", split_axis=0, concat_axis=0, tiled=True)

    fields = [
        pltpu.with_memory_space_constraint(x, pltpu.HBM)
        for x in (tracer, thickness, wind_u, wind_v)
    ]
    to_first, to_second, kept = call(
        edge_kernel,
        [HB] * 4,
        [(VM, halo), (VM, halo), (VM, (7, 8, LON))],
        scratch=[pltpu.VMEM((4, 2, 4, LON), f32), pltpu.SemaphoreType.DMA((8,))],
    )(*fields)
    lev_count = lax.axis_size("lev")
    moves = []
    for start in (1, 0):
        pairs = [(i, i + 1) for i in range(start, lat_count - 1, 2)]
        lats = dict(pairs + [(b, a) for a, b in pairs])
        moves.append(
            [
                (lat * lev_count + lev, lats[lat] * lev_count + lev if lat in lats else lat * lev_count + (lev ^ 1))
                for lat in range(lat_count)
                for lev in range(lev_count)
            ]
        )
    first_halo, second_halo = [
        lax.ppermute(rows, ("lat", "lev"), move) for rows, move in zip((to_first, to_second), moves)
    ]
    send, edges = call(
        first_kernel,
        [VM] * 4,
        [(VM, chunks), (VM, (2, 8, LON))],
        scratch=[pltpu.VMEM((2,) + slab, f32)],
    )(tracer, thickness, wind_u, wind_v)
    factors = call(
        factor_kernel,
        [VM, VM],
        [(VM, (3, LEVELS, ROWS, LANES)), (VM, (3, LEVELS, 8, LANES))],
    )(offsets, coupling)
    edges, *factors = lax.optimization_barrier((edges, *factors))
    (send,) = call(
        second_kernel,
        [VM] * 4 + [ANY],
        [(ANY, chunks)],
        scratch=[
            pltpu.VMEM((2, 8, LON), f32),
            pltpu.VMEM((DEST, 72, LANES), f32),
            pltpu.SemaphoreType.DMA((9,)),
        ],
        aliases={4: 0},
    )(first_halo, second_halo, kept, edges, send)
    received = transposed(send)
    (back,) = call(column_kernel, [VM] * 3, [(VM, (DEST, 112, LANES))])(received, *factors)
    returned = transposed(back)
    return tuple(
        call(
            unpack_kernel,
            [VM],
            [(ANY, slab)] * 3,
            scratch=[pltpu.VMEM((3,) + slab, f32), pltpu.SemaphoreType.DMA((6,))],
        )(returned)
    )


def solution(mesh):
    return jax.shard_map(
        local,
        mesh=mesh,
        in_specs=(
            P("lev", "lat", None),
            P("lev", "lat", None),
            P("lev", "lat", None),
            P("lev", "lat", None),
            P(None, "lat", "lev"),
            P(None, "lat", "lev"),
        ),
        out_specs=(P("lev", "lat", None), P("lev", "lat", None), P("lev", "lat", None)),
        check_vma=False,
    )
```

```python
import jax
import jax.numpy as jnp
from jax import lax
from jax.experimental import pallas as pl
from jax.experimental.pallas import tpu as pltpu
from jax.sharding import PartitionSpec as P

courant_max = 0.24
LEVELS = 32
LON = 2304
ROWS = 16
DEST = 16
COLS = 144
LANES = 128
VM = pl.BlockSpec(memory_space=pltpu.VMEM)
ANY = pl.BlockSpec(memory_space=pl.ANY)
HB = pl.BlockSpec(memory_space=pltpu.HBM)
PARAMS = pltpu.CompilerParams(vmem_limit_bytes=24 * 1024 * 1024)


def lane_ids(rows):
    return lax.broadcasted_iota(jnp.int32, (rows, LANES), 1)


def row_ids(rows):
    return lax.broadcasted_iota(jnp.int32, (rows, LON), 0)


def courant(pair_sum):
    return courant_max * jnp.tanh(0.5 * pair_sum)


def upwind(flow, before, after):
    return jnp.maximum(flow, 0.0) * before + jnp.minimum(flow, 0.0) * after


def east_roll(x):
    return pltpu.roll(x, 1, 1)


def west_roll(x):
    return pltpu.roll(x, LON - 1, 1)


def zonal(east, mass):
    flux = upwind(east, east_roll(mass), mass)
    return flux - west_roll(flux)


def edge_kernel(tracer, thickness, wind_u, wind_v, to_first, to_second, kept, fetched, sems):
    copies = [
        pltpu.make_async_copy(
            ref.at[:, pl.ds(14 * end, 2), :],
            fetched.at[slot, :, pl.ds(2 * end, 2), :],
            sems.at[2 * slot + end],
        )
        for slot, ref in enumerate((tracer, thickness, wind_u, wind_v))
        for end in range(2)
    ]
    for copy in copies:
        copy.start()
    for copy in copies:
        copy.wait()
    tracer, layer, u, v = [
        jnp.concatenate(
            [fetched[slot, 0, 0:2], fetched[slot, 1, 2:4], fetched[slot, 1, 0:2], fetched[slot, 0, 2:4]],
            axis=0,
        )
        for slot in range(4)
    ]
    mass = tracer * layer
    east = courant(east_roll(u) + u)
    north = courant(v + pltpu.roll(v, 7, 0))
    odd = lax.rem(row_ids(8), 2) == 1
    upper = lax.rem(row_ids(8), 4) >= 2
    inner = jnp.where(odd, pltpu.roll(north, 1, 0), north)

    def partial(m):
        flux = upwind(north, m, pltpu.roll(m, 7, 0))
        return m + zonal(east, m) + jnp.where(odd, pltpu.roll(flux, 1, 0), -flux)

    values = (v, mass, layer, partial(mass), partial(layer))
    odd_lat = lax.rem(lax.axis_index("lat"), 2) == 1
    north_first = jnp.broadcast_to(odd_lat, (1, LON))
    for slot, value in enumerate(values):
        for level in range(2):
            south = value[4 * level : 4 * level + 1]
            north_row = value[7 - 4 * level : 8 - 4 * level]
            to_first[slot, level : level + 1, :] = jnp.where(north_first, north_row, south)
            to_second[slot, level : level + 1, :] = jnp.where(north_first, south, north_row)
        kept[slot] = value
    kept[5] = east
    kept[6] = jnp.where(upper, jnp.minimum(inner, 0.0), -jnp.maximum(inner, 0.0))
    kept[7] = u


def first_kernel(tracer, thickness, wind_u, wind_v, send, edges, held):
    row = row_ids(ROWS)
    for level in range(2):
        u, v, layer = wind_u[level], wind_v[level], thickness[level]
        mass = tracer[level] * layer
        east = courant(east_roll(u) + u)
        north = jnp.where(row == 0, 0.0, courant(pltpu.roll(v, 1, 0) + v))
        done = []
        for slot, m in enumerate((mass, layer)):
            for substep in range(2):
                flux = upwind(north, pltpu.roll(m, 1, 0), m)
                above = jnp.where(row == ROWS - 1, 0.0, pltpu.roll(flux, ROWS - 1, 0))
                m = m + zonal(east, m) + flux - above
            edges[slot, 4 * level : 4 * level + 2, :] = m[0:2]
            edges[slot, 6 - 4 * level : 8 - 4 * level, :] = m[14:16]
            done.append(m)
        mass, layer = done
        for field, m in enumerate((mass, layer * u, layer * v, layer)):
            held[field, level] = m
    lane = lane_ids(ROWS)
    lane8 = lane_ids(8)
    for dest in range(DEST):
        tile = dest + dest // 8
        shift = 16 * (dest % 8)
        low = slice(tile * LANES, (tile + 1) * LANES)
        high = slice((tile + 1) * LANES, (tile + 2) * LANES)
        for level in range(2):
            packed = None
            for field in range(4):
                here = held[field, level, :, low]
                after = held[field, level, :, high]
                block = here if shift == 0 else jnp.where(lane >= shift, here, after)
                start = (field * 2 + level) * ROWS
                send[dest, start : start + ROWS, :] = block
                for half in range(2):
                    part = after[8 * half : 8 * half + 8]
                    part = pltpu.roll(part, 2, 0) if half else part
                    place = 32 * field + 16 * half
                    part = pltpu.roll(part, (place - shift) % LANES, 1)
                    packed = part if packed is None else jnp.where(lane8 >= place, part, packed)
            send[dest, 128 + 8 * level : 136 + 8 * level, :] = packed


def second_kernel(first_halo, second_halo, kept, edges, sent, send, held):
    lat = lax.axis_index("lat")
    row = lax.rem(row_ids(8), 4)
    upper = row >= 2
    outer = (row == 0) | (row == 3)
    even = jnp.broadcast_to(lax.rem(lat, 2) == 0, (1, LON))
    south_open = jnp.where(lat > 0, 1.0, 0.0)
    north_open = jnp.where(lat < lax.axis_size("lat") - 1, 1.0, 0.0)
    open_face = jnp.where(upper, north_open, south_open)

    def halo(slot):
        south, north = [], []
        for level in range(2):
            one = first_halo[slot, level : level + 1, :]
            two = second_halo[slot, level : level + 1, :]
            south.append(jnp.where(even, one, two))
            north.append(jnp.where(even, two, one))
        rows = [jnp.where(upper[0:4], north[1 - level], south[level]) for level in range(2)]
        return jnp.concatenate(rows, axis=0)

    v, east, inner = kept[0], kept[5], kept[6]
    flow = open_face * courant(v + halo(0))
    sign = jnp.where(upper, -1.0, 1.0)
    done = []
    for slot in range(2):
        m, m_beyond = kept[1 + slot], halo(1 + slot)
        partial, beyond = kept[3 + slot], halo(3 + slot)
        flux = upwind(flow, jnp.where(upper, m, m_beyond), jnp.where(upper, m_beyond, m))
        change = jnp.where(outer, sign * flux, 0.0)
        partial = partial + change
        beyond = beyond - change
        flux = upwind(flow, jnp.where(upper, partial, beyond), jnp.where(upper, beyond, partial))
        carried = inner * change
        gain = change + zonal(east, change) + carried + sign * flux
        passed = jnp.where(row == 1, pltpu.roll(carried, 1, 0), pltpu.roll(carried, 7, 0))
        done.append(edges[slot] + jnp.where(outer, gain, -passed))
    mass, layer = done
    for field, m in enumerate((mass, layer * kept[7], layer * v, layer)):
        held[field] = m
    lane = lane_ids(8)
    upper_half = lax.rem(lane, 32) >= 16
    place = lax.broadcasted_iota(jnp.int32, (8, LANES), 0)
    low_ends, high_ends = place < 2, place >= 6
    for dest in range(DEST):
        tile = dest + dest // 8
        shift = 16 * (dest % 8)
        low = slice(tile * LANES, (tile + 1) * LANES)
        high = slice((tile + 1) * LANES, (tile + 2) * LANES)
        halves = [None, None]
        for field in range(4):
            here, after = held[field, :, low], held[field, :, high]
            block = here if shift == 0 else jnp.where(lane >= shift, here, after)
            for level in range(2):
                ends = pltpu.roll(block, 4, 0) if level else block
                start = (field * 2 + level) * ROWS
                rows = sent[dest, start : start + 8, :]
                send[dest, start : start + 8, :] = jnp.where(low_ends, ends, rows)
                rows = sent[dest, start + 8 : start + 16, :]
                send[dest, start + 8 : start + 16, :] = jnp.where(high_ends, ends, rows)
            for half in range(2):
                part = pltpu.roll(after, (32 * field + 16 * half - shift) % LANES, 1)
                halves[half] = jnp.where(lane >= 32 * field, part, halves[half]) if field else part
        first, last = halves
        for level, ends in enumerate(
            (
                jnp.where(upper_half, pltpu.roll(last, 2, 0), first),
                jnp.where(upper_half, pltpu.roll(last, 6, 0), pltpu.roll(first, 4, 0)),
            )
        ):
            start = 128 + 8 * level
            rows = sent[dest, start : start + 8, :]
            send[dest, start : start + 8, :] = jnp.where(low_ends, ends, rows)


def factor_kernel(offsets, coupling, factors_main, factors_rest):
    shift = 16 * lax.rem(lax.axis_index("lev"), 8)
    half = lax.rem(lane_ids(8), 32) >= 16

    def main(ref, k):
        return pltpu.roll(ref[k, :, 0:LANES], shift, 1)

    def rest(ref, k):
        part = ref[k, :, LANES:COLS]
        both = jnp.concatenate([part[0:8], part[8:16]], axis=1)
        all_fields = jnp.concatenate([both, both, both, both], axis=1)
        return jnp.where(half, pltpu.roll(all_fields, 2, 0), all_fields)

    for load, factors, shape in (
        (main, factors_main, (ROWS, LANES)),
        (rest, factors_rest, (8, LANES)),
    ):
        low = jnp.zeros(shape, jnp.float32)
        back = jnp.zeros(shape, jnp.float32)
        for k in range(LEVELS):
            choose = load(offsets, k)
            high = load(coupling, k) if k < LEVELS - 1 else jnp.zeros(shape, jnp.float32)
            scale = 1.0 / (1.0 + low + high - low * back)
            back = high * scale
            factors[0, k] = jnp.where(choose == 0, -scale, scale)
            factors[1, k] = low * scale
            factors[2, k] = jnp.where(choose == 2, -back, back)
            low = high


def column_kernel(received, factors_main, factors_rest, send):
    lane = lane_ids(8)

    def main(k):
        base = (k % 2) * ROWS
        return [received[k // 2, base + 32 * f : base + 32 * f + ROWS, :] for f in range(4)]

    def rest(k):
        base = 128 + 8 * (k % 2)
        return received[k // 2, base : base + 8, :]

    def picked(below, above, sums):
        return jnp.where(below, sums[0], jnp.where(above, sums[2], sums[1]))

    solve_main = [jnp.zeros((ROWS, LANES), jnp.float32)] * 3
    solve_rest = jnp.zeros((8, LANES), jnp.float32)
    main_here, rest_here = main(0), rest(0)
    main_sums, rest_sums = [], []

    def push(k):
        nonlocal main_here, rest_here
        main_next, rest_next = main(k + 1), rest(k + 1)
        main_sums.append([a + b for a, b in zip(main_here, main_next)])
        rest_sums.append(rest_here + rest_next)
        main_here, rest_here = main_next, rest_next

    push(0)
    for k in range(LEVELS):
        if k + 1 < LEVELS - 1:
            push(k + 1)
        three = [max(k - 1, 0), min(k, LEVELS - 2), min(k + 1, LEVELS - 2)]
        scale = factors_main[0, k]
        below, above = scale < 0.0, factors_main[2, k] < 0.0
        values = [picked(below, above, [main_sums[i][f] for i in three]) for f in range(4)]
        weight = jnp.abs(scale) / values[3]
        low = factors_main[1, k]
        solve_main = [values[f] * weight + low * solve_main[f] for f in range(3)]
        for f in range(3):
            base = (f * 2 + k % 2) * ROWS
            send[k // 2, base : base + ROWS, :] = solve_main[f]
        scale = factors_rest[0, k]
        below, above = scale < 0.0, factors_rest[2, k] < 0.0
        value = picked(below, above, [rest_sums[i] for i in three])
        total = jnp.where(lane >= 64, pltpu.roll(value, 96, 1), pltpu.roll(value, 32, 1))
        total = jnp.where(lane >= 32, jnp.where(lane >= 64, total, pltpu.roll(value, 64, 1)), total)
        solve_rest = value * (jnp.abs(scale) / total) + factors_rest[1, k] * solve_rest
        base = 96 + 8 * (k % 2)
        send[k // 2, base : base + 8, :] = solve_rest
    for k in range(LEVELS - 2, -1, -1):
        back = jnp.abs(factors_main[2, k])
        for f in range(3):
            base = (f * 2 + k % 2) * ROWS
            solve_main[f] = send[k // 2, base : base + ROWS, :] + back * solve_main[f]
            send[k // 2, base : base + ROWS, :] = solve_main[f]
        base = 96 + 8 * (k % 2)
        solve_rest = send[k // 2, base : base + 8, :] + jnp.abs(factors_rest[2, k]) * solve_rest
        send[k // 2, base : base + 8, :] = solve_rest


def unpack_kernel(received, tracer_out, u_out, v_out, whole, sems):
    lane = lane_ids(ROWS)
    copies = []
    for field, out in enumerate((tracer_out, u_out, v_out)):
        for level in range(2):
            base = (field * 2 + level) * ROWS
            for tile in range(LON // LANES):
                source = tile if tile < 8 else tile - 1
                fresh = tile != 8 and tile != 17
                shift = 16 * (source % 8) if fresh else LANES
                value = received[source, base : base + ROWS, :] if fresh else None
                if shift > 0:
                    last = source - 1 if fresh else (7 if tile == 8 else 15)
                    place = shift - 16
                    packed = received[last, 96 + 8 * level : 104 + 8 * level, :]
                    start = place - 32 * field
                    rest = jnp.concatenate(
                        [
                            pltpu.roll(packed, start % LANES, 1),
                            pltpu.roll(pltpu.roll(packed, 6, 0), (start - 16) % LANES, 1),
                        ],
                        axis=0,
                    )
                    old = received[last, base : base + ROWS, :]
                    old = jnp.where(lane >= place, rest, old) if place > 0 else rest
                    value = jnp.where(lane >= shift, value, old) if fresh else old
                whole[field, level, :, tile * LANES : (tile + 1) * LANES] = value
            copy = pltpu.make_async_copy(
                whole.at[field, level], out.at[level], sems.at[2 * field + level]
            )
            copy.start()
            copies.append(copy)
    for copy in copies:
        copy.wait()


def call(kernel, in_specs, outs, scratch=(), aliases=None, flops=1000000, nbytes=3000000):
    return pl.pallas_call(
        kernel,
        in_specs=in_specs,
        out_specs=[spec for spec, _ in outs],
        out_shape=[jax.ShapeDtypeStruct(shape, jnp.float32) for _, shape in outs],
        scratch_shapes=scratch,
        input_output_aliases=aliases or {},
        compiler_params=PARAMS,
        cost_estimate=pl.CostEstimate(flops=flops, bytes_accessed=nbytes, transcendentals=0),
    )


def local(tracer, thickness, wind_u, wind_v, offsets, coupling):
    f32 = jnp.float32
    lat_count = lax.axis_size("lat")
    slab = (2, ROWS, LON)
    halo = (5, 2, LON)
    chunks = (DEST, 144, LANES)

    def transposed(block):
        return lax.all_to_all(block, "lev", split_axis=0, concat_axis=0, tiled=True)

    fields = [
        pltpu.with_memory_space_constraint(x, pltpu.HBM)
        for x in (tracer, thickness, wind_u, wind_v)
    ]
    to_first, to_second, kept = call(
        edge_kernel,
        [HB] * 4,
        [(VM, halo), (VM, halo), (VM, (8, 8, LON))],
        scratch=[pltpu.VMEM((4, 2, 4, LON), f32), pltpu.SemaphoreType.DMA((8,))],
    )(*fields)
    lev_count = lax.axis_size("lev")
    moves = []
    for start in (1, 0):
        pairs = [(i, i + 1) for i in range(start, lat_count - 1, 2)]
        lats = dict(pairs + [(b, a) for a, b in pairs])
        moves.append(
            [
                (lat * lev_count + lev, lats[lat] * lev_count + lev if lat in lats else lat * lev_count + (lev ^ 1))
                for lat in range(lat_count)
                for lev in range(lev_count)
            ]
        )
    first_halo, second_halo = [
        lax.ppermute(rows, ("lat", "lev"), move) for rows, move in zip((to_first, to_second), moves)
    ]
    send, edges = call(
        first_kernel,
        [VM] * 4,
        [(VM, chunks), (VM, (2, 8, LON))],
        scratch=[pltpu.VMEM((4,) + slab, f32)],
    )(tracer, thickness, wind_u, wind_v)
    factors = call(
        factor_kernel,
        [VM, VM],
        [(VM, (3, LEVELS, ROWS, LANES)), (VM, (3, LEVELS, 8, LANES))],
    )(offsets, coupling)
    edges, *factors = lax.optimization_barrier((edges, *factors))
    (send,) = call(
        second_kernel,
        [VM] * 5,
        [(VM, chunks)],
        scratch=[pltpu.VMEM((4, 8, LON), f32)],
    )(first_halo, second_halo, kept, edges, send)
    received = transposed(send)
    (back,) = call(column_kernel, [VM] * 3, [(VM, (DEST, 112, LANES))])(received, *factors)
    returned = transposed(back)
    return tuple(
        call(
            unpack_kernel,
            [VM],
            [(ANY, slab)] * 3,
            scratch=[pltpu.VMEM((3,) + slab, f32), pltpu.SemaphoreType.DMA((6,))],
        )(returned)
    )


def solution(mesh):
    return jax.shard_map(
        local,
        mesh=mesh,
        in_specs=(
            P("lev", "lat", None),
            P("lev", "lat", None),
            P("lev", "lat", None),
            P("lev", "lat", None),
            P(None, "lat", "lev"),
            P(None, "lat", "lev"),
        ),
        out_specs=(P("lev", "lat", None), P("lev", "lat", None), P("lev", "lat", None)),
        check_vma=False,
    )
```

```python
import jax
import jax.numpy as jnp
from jax import lax
from jax.experimental import pallas as pl
from jax.experimental.pallas import tpu as pltpu
from jax.sharding import PartitionSpec as P

courant_max = 0.24
LEVELS = 32
LON = 2304
ROWS = 16
DEST = 16
COLS = 144
LANES = 128
VM = pl.BlockSpec(memory_space=pltpu.VMEM)
ANY = pl.BlockSpec(memory_space=pl.ANY)
HB = pl.BlockSpec(memory_space=pltpu.HBM)
PARAMS = pltpu.CompilerParams(vmem_limit_bytes=24 * 1024 * 1024)


def lane_ids(rows):
    return lax.broadcasted_iota(jnp.int32, (rows, LANES), 1)


def row_ids(rows):
    return lax.broadcasted_iota(jnp.int32, (rows, LON), 0)


def courant(pair_sum):
    return courant_max * jnp.tanh(0.5 * pair_sum)


def upwind(flow, before, after):
    return jnp.maximum(flow, 0.0) * before + jnp.minimum(flow, 0.0) * after


def east_roll(x):
    return pltpu.roll(x, 1, 1)


def west_roll(x):
    return pltpu.roll(x, LON - 1, 1)


def zonal(east, mass):
    flux = upwind(east, east_roll(mass), mass)
    return flux - west_roll(flux)


def edge_kernel(tracer, thickness, wind_u, wind_v, to_first, to_second, fetched, sems):
    copies = [
        pltpu.make_async_copy(
            ref.at[:, pl.ds(14 * end, 2), :],
            fetched.at[slot, :, pl.ds(2 * end, 2), :],
            sems.at[2 * slot + end],
        )
        for slot, ref in enumerate((tracer, thickness, wind_u, wind_v))
        for end in range(2)
    ]
    for copy in copies:
        copy.start()
    for copy in copies:
        copy.wait()
    tracer, layer, u, v = [
        jnp.concatenate(
            [fetched[slot, 0, 0:2], fetched[slot, 1, 2:4], fetched[slot, 1, 0:2], fetched[slot, 0, 2:4]],
            axis=0,
        )
        for slot in range(4)
    ]
    mass = tracer * layer
    east = courant(east_roll(u) + u)
    north = courant(v + pltpu.roll(v, 7, 0))
    odd = lax.rem(row_ids(8), 2) == 1

    def partial(m):
        flux = upwind(north, m, pltpu.roll(m, 7, 0))
        return m + zonal(east, m) + jnp.where(odd, pltpu.roll(flux, 1, 0), -flux)

    values = (v, mass, layer, partial(mass), partial(layer))
    odd_lat = lax.rem(lax.axis_index("lat"), 2) == 1
    north_first = jnp.broadcast_to(odd_lat, (1, LON))
    for slot, value in enumerate(values):
        for level in range(2):
            south = value[4 * level : 4 * level + 1]
            north_row = value[7 - 4 * level : 8 - 4 * level]
            to_first[slot, level : level + 1, :] = jnp.where(north_first, north_row, south)
            to_second[slot, level : level + 1, :] = jnp.where(north_first, south, north_row)


def first_kernel(tracer, thickness, wind_u, wind_v, send, kept, edges, held):
    row = row_ids(ROWS)
    for level in range(2):
        u, v, layer = wind_u[level], wind_v[level], thickness[level]
        mass = tracer[level] * layer
        east = courant(east_roll(u) + u)
        north = jnp.where(row == 0, 0.0, courant(pltpu.roll(v, 1, 0) + v))
        low, high = slice(4 * level, 4 * level + 2), slice(6 - 4 * level, 8 - 4 * level)

        def keep(slot, value):
            kept[slot, low, :] = value[0:2]
            kept[slot, high, :] = value[14:16]

        keep(0, v)
        keep(5, east)
        keep(7, u)
        kept[6, low, :] = jnp.broadcast_to(-jnp.maximum(north[1:2], 0.0), (2, LON))
        kept[6, high, :] = jnp.broadcast_to(jnp.minimum(north[15:16], 0.0), (2, LON))
        done = []
        for slot, m in enumerate((mass, layer)):
            keep(1 + slot, m)
            for substep in range(2):
                flux = upwind(north, pltpu.roll(m, 1, 0), m)
                above = jnp.where(row == ROWS - 1, 0.0, pltpu.roll(flux, ROWS - 1, 0))
                m = m + zonal(east, m) + flux - above
                if substep == 0:
                    keep(3 + slot, m)
            edges[slot, low, :] = m[0:2]
            edges[slot, high, :] = m[14:16]
            done.append(m)
        mass, layer = done
        for field, m in enumerate((mass, layer * u, layer * v, layer)):
            held[field, level] = m
    lane = lane_ids(ROWS)
    lane8 = lane_ids(8)
    for dest in range(DEST):
        tile = dest + dest // 8
        shift = 16 * (dest % 8)
        low = slice(tile * LANES, (tile + 1) * LANES)
        high = slice((tile + 1) * LANES, (tile + 2) * LANES)
        for level in range(2):
            packed = None
            for field in range(4):
                here = held[field, level, :, low]
                after = held[field, level, :, high]
                block = here if shift == 0 else jnp.where(lane >= shift, here, after)
                start = (field * 2 + level) * ROWS
                send[dest, start : start + ROWS, :] = block
                for half in range(2):
                    part = after[8 * half : 8 * half + 8]
                    part = pltpu.roll(part, 2, 0) if half else part
                    place = 32 * field + 16 * half
                    part = pltpu.roll(part, (place - shift) % LANES, 1)
                    packed = part if packed is None else jnp.where(lane8 >= place, part, packed)
            send[dest, 128 + 8 * level : 136 + 8 * level, :] = packed


def second_kernel(first_halo, second_halo, kept, edges, sent, send, held):
    lat = lax.axis_index("lat")
    row = lax.rem(row_ids(8), 4)
    upper = row >= 2
    outer = (row == 0) | (row == 3)
    even = jnp.broadcast_to(lax.rem(lat, 2) == 0, (1, LON))
    south_open = jnp.where(lat > 0, 1.0, 0.0)
    north_open = jnp.where(lat < lax.axis_size("lat") - 1, 1.0, 0.0)
    open_face = jnp.where(upper, north_open, south_open)

    def halo(slot):
        south, north = [], []
        for level in range(2):
            one = first_halo[slot, level : level + 1, :]
            two = second_halo[slot, level : level + 1, :]
            south.append(jnp.where(even, one, two))
            north.append(jnp.where(even, two, one))
        rows = [jnp.where(upper[0:4], north[1 - level], south[level]) for level in range(2)]
        return jnp.concatenate(rows, axis=0)

    v, east, inner = kept[0], kept[5], kept[6]
    flow = open_face * courant(v + halo(0))
    sign = jnp.where(upper, -1.0, 1.0)
    done = []
    for slot in range(2):
        m, m_beyond = kept[1 + slot], halo(1 + slot)
        partial, beyond = kept[3 + slot], halo(3 + slot)
        flux = upwind(flow, jnp.where(upper, m, m_beyond), jnp.where(upper, m_beyond, m))
        change = jnp.where(outer, sign * flux, 0.0)
        partial = partial + change
        beyond = beyond - change
        flux = upwind(flow, jnp.where(upper, partial, beyond), jnp.where(upper, beyond, partial))
        carried = inner * change
        gain = change + zonal(east, change) + carried + sign * flux
        passed = jnp.where(row == 1, pltpu.roll(carried, 1, 0), pltpu.roll(carried, 7, 0))
        done.append(edges[slot] + jnp.where(outer, gain, -passed))
    mass, layer = done
    for field, m in enumerate((mass, layer * kept[7], layer * v, layer)):
        held[field] = m
    lane = lane_ids(8)
    upper_half = lax.rem(lane, 32) >= 16
    place = lax.broadcasted_iota(jnp.int32, (8, LANES), 0)
    low_ends, high_ends = place < 2, place >= 6
    for dest in range(DEST):
        tile = dest + dest // 8
        shift = 16 * (dest % 8)
        low = slice(tile * LANES, (tile + 1) * LANES)
        high = slice((tile + 1) * LANES, (tile + 2) * LANES)
        halves = [None, None]
        for field in range(4):
            here, after = held[field, :, low], held[field, :, high]
            block = here if shift == 0 else jnp.where(lane >= shift, here, after)
            for level in range(2):
                ends = pltpu.roll(block, 4, 0) if level else block
                start = (field * 2 + level) * ROWS
                rows = sent[dest, start : start + 8, :]
                send[dest, start : start + 8, :] = jnp.where(low_ends, ends, rows)
                rows = sent[dest, start + 8 : start + 16, :]
                send[dest, start + 8 : start + 16, :] = jnp.where(high_ends, ends, rows)
            for half in range(2):
                part = pltpu.roll(after, (32 * field + 16 * half - shift) % LANES, 1)
                halves[half] = jnp.where(lane >= 32 * field, part, halves[half]) if field else part
        first, last = halves
        for level, ends in enumerate(
            (
                jnp.where(upper_half, pltpu.roll(last, 2, 0), first),
                jnp.where(upper_half, pltpu.roll(last, 6, 0), pltpu.roll(first, 4, 0)),
            )
        ):
            start = 128 + 8 * level
            rows = sent[dest, start : start + 8, :]
            send[dest, start : start + 8, :] = jnp.where(low_ends, ends, rows)


def factor_kernel(offsets, coupling, factors_main, factors_rest):
    shift = 16 * lax.rem(lax.axis_index("lev"), 8)
    half = lax.rem(lane_ids(8), 32) >= 16

    def main(ref, k):
        return pltpu.roll(ref[k, :, 0:LANES], shift, 1)

    def rest(ref, k):
        part = ref[k, :, LANES:COLS]
        both = jnp.concatenate([part[0:8], part[8:16]], axis=1)
        all_fields = jnp.concatenate([both, both, both, both], axis=1)
        return jnp.where(half, pltpu.roll(all_fields, 2, 0), all_fields)

    for load, factors, shape in (
        (main, factors_main, (ROWS, LANES)),
        (rest, factors_rest, (8, LANES)),
    ):
        low = jnp.zeros(shape, jnp.float32)
        back = jnp.zeros(shape, jnp.float32)
        for k in range(LEVELS):
            choose = load(offsets, k)
            high = load(coupling, k) if k < LEVELS - 1 else jnp.zeros(shape, jnp.float32)
            scale = 1.0 / (1.0 + low + high - low * back)
            back = high * scale
            factors[0, k] = jnp.where(choose == 0, -scale, scale)
            factors[1, k] = low * scale
            factors[2, k] = jnp.where(choose == 2, -back, back)
            low = high


def column_kernel(received, factors_main, factors_rest, send):
    lane = lane_ids(8)

    def main(k):
        base = (k % 2) * ROWS
        return [received[k // 2, base + 32 * f : base + 32 * f + ROWS, :] for f in range(4)]

    def rest(k):
        base = 128 + 8 * (k % 2)
        return received[k // 2, base : base + 8, :]

    def picked(below, above, sums):
        return jnp.where(below, sums[0], jnp.where(above, sums[2], sums[1]))

    solve_main = [jnp.zeros((ROWS, LANES), jnp.float32)] * 3
    solve_rest = jnp.zeros((8, LANES), jnp.float32)
    main_here, rest_here = main(0), rest(0)
    main_sums, rest_sums = [], []

    def push(k):
        nonlocal main_here, rest_here
        main_next, rest_next = main(k + 1), rest(k + 1)
        main_sums.append([a + b for a, b in zip(main_here, main_next)])
        rest_sums.append(rest_here + rest_next)
        main_here, rest_here = main_next, rest_next

    push(0)
    for k in range(LEVELS):
        if k + 1 < LEVELS - 1:
            push(k + 1)
        three = [max(k - 1, 0), min(k, LEVELS - 2), min(k + 1, LEVELS - 2)]
        scale = factors_main[0, k]
        below, above = scale < 0.0, factors_main[2, k] < 0.0
        values = [picked(below, above, [main_sums[i][f] for i in three]) for f in range(4)]
        weight = jnp.abs(scale) / values[3]
        low = factors_main[1, k]
        solve_main = [values[f] * weight + low * solve_main[f] for f in range(3)]
        for f in range(3):
            base = (f * 2 + k % 2) * ROWS
            send[k // 2, base : base + ROWS, :] = solve_main[f]
        scale = factors_rest[0, k]
        below, above = scale < 0.0, factors_rest[2, k] < 0.0
        value = picked(below, above, [rest_sums[i] for i in three])
        total = jnp.where(lane >= 64, pltpu.roll(value, 96, 1), pltpu.roll(value, 32, 1))
        total = jnp.where(lane >= 32, jnp.where(lane >= 64, total, pltpu.roll(value, 64, 1)), total)
        solve_rest = value * (jnp.abs(scale) / total) + factors_rest[1, k] * solve_rest
        base = 96 + 8 * (k % 2)
        send[k // 2, base : base + 8, :] = solve_rest
    for k in range(LEVELS - 2, -1, -1):
        back = jnp.abs(factors_main[2, k])
        for f in range(3):
            base = (f * 2 + k % 2) * ROWS
            solve_main[f] = send[k // 2, base : base + ROWS, :] + back * solve_main[f]
            send[k // 2, base : base + ROWS, :] = solve_main[f]
        base = 96 + 8 * (k % 2)
        solve_rest = send[k // 2, base : base + 8, :] + jnp.abs(factors_rest[2, k]) * solve_rest
        send[k // 2, base : base + 8, :] = solve_rest


def unpack_kernel(received, tracer_out, u_out, v_out, whole, sems):
    lane = lane_ids(ROWS)
    copies = []
    for field, out in enumerate((tracer_out, u_out, v_out)):
        for level in range(2):
            base = (field * 2 + level) * ROWS
            for tile in range(LON // LANES):
                source = tile if tile < 8 else tile - 1
                fresh = tile != 8 and tile != 17
                shift = 16 * (source % 8) if fresh else LANES
                value = received[source, base : base + ROWS, :] if fresh else None
                if shift > 0:
                    last = source - 1 if fresh else (7 if tile == 8 else 15)
                    place = shift - 16
                    packed = received[last, 96 + 8 * level : 104 + 8 * level, :]
                    start = place - 32 * field
                    rest = jnp.concatenate(
                        [
                            pltpu.roll(packed, start % LANES, 1),
                            pltpu.roll(pltpu.roll(packed, 6, 0), (start - 16) % LANES, 1),
                        ],
                        axis=0,
                    )
                    old = received[last, base : base + ROWS, :]
                    old = jnp.where(lane >= place, rest, old) if place > 0 else rest
                    value = jnp.where(lane >= shift, value, old) if fresh else old
                whole[field, level, :, tile * LANES : (tile + 1) * LANES] = value
            copy = pltpu.make_async_copy(
                whole.at[field, level], out.at[level], sems.at[2 * field + level]
            )
            copy.start()
            copies.append(copy)
    for copy in copies:
        copy.wait()


def call(kernel, in_specs, outs, scratch=(), aliases=None, flops=1000000, nbytes=3000000):
    return pl.pallas_call(
        kernel,
        in_specs=in_specs,
        out_specs=[spec for spec, _ in outs],
        out_shape=[jax.ShapeDtypeStruct(shape, jnp.float32) for _, shape in outs],
        scratch_shapes=scratch,
        input_output_aliases=aliases or {},
        compiler_params=PARAMS,
        cost_estimate=pl.CostEstimate(flops=flops, bytes_accessed=nbytes, transcendentals=0),
    )


def local(tracer, thickness, wind_u, wind_v, offsets, coupling):
    f32 = jnp.float32
    lat_count = lax.axis_size("lat")
    slab = (2, ROWS, LON)
    halo = (5, 2, LON)
    chunks = (DEST, 144, LANES)

    def transposed(block):
        return lax.all_to_all(block, "lev", split_axis=0, concat_axis=0, tiled=True)

    fields = [
        pltpu.with_memory_space_constraint(x, pltpu.HBM)
        for x in (tracer, thickness, wind_u, wind_v)
    ]
    to_first, to_second = call(
        edge_kernel,
        [HB] * 4,
        [(VM, halo), (VM, halo)],
        scratch=[pltpu.VMEM((4, 2, 4, LON), f32), pltpu.SemaphoreType.DMA((8,))],
    )(*fields)
    lev_count = lax.axis_size("lev")
    moves = []
    for start in (1, 0):
        pairs = [(i, i + 1) for i in range(start, lat_count - 1, 2)]
        lats = dict(pairs + [(b, a) for a, b in pairs])
        moves.append(
            [
                (lat * lev_count + lev, lats[lat] * lev_count + lev if lat in lats else lat * lev_count + (lev ^ 1))
                for lat in range(lat_count)
                for lev in range(lev_count)
            ]
        )
    first_halo, second_halo = [
        lax.ppermute(rows, ("lat", "lev"), move) for rows, move in zip((to_first, to_second), moves)
    ]
    send, kept, edges = call(
        first_kernel,
        [VM] * 4,
        [(VM, chunks), (VM, (8, 8, LON)), (VM, (2, 8, LON))],
        scratch=[pltpu.VMEM((4,) + slab, f32)],
    )(tracer, thickness, wind_u, wind_v)
    factors = call(
        factor_kernel,
        [VM, VM],
        [(VM, (3, LEVELS, ROWS, LANES)), (VM, (3, LEVELS, 8, LANES))],
    )(offsets, coupling)
    edges, *factors = lax.optimization_barrier((edges, *factors))
    (send,) = call(
        second_kernel,
        [VM] * 5,
        [(VM, chunks)],
        scratch=[pltpu.VMEM((4, 8, LON), f32)],
    )(first_halo, second_halo, kept, edges, send)
    received = transposed(send)
    (back,) = call(column_kernel, [VM] * 3, [(VM, (DEST, 112, LANES))])(received, *factors)
    returned = transposed(back)
    return tuple(
        call(
            unpack_kernel,
            [VM],
            [(ANY, slab)] * 3,
            scratch=[pltpu.VMEM((3,) + slab, f32), pltpu.SemaphoreType.DMA((6,))],
        )(returned)
    )


def solution(mesh):
    return jax.shard_map(
        local,
        mesh=mesh,
        in_specs=(
            P("lev", "lat", None),
            P("lev", "lat", None),
            P("lev", "lat", None),
            P("lev", "lat", None),
            P(None, "lat", "lev"),
            P(None, "lat", "lev"),
        ),
        out_specs=(P("lev", "lat", None), P("lev", "lat", None), P("lev", "lat", None)),
        check_vma=False,
    )
```

```python
import jax
import jax.numpy as jnp
from jax import lax
from jax.experimental import pallas as pl
from jax.experimental.pallas import tpu as pltpu
from jax.sharding import PartitionSpec as P

courant_max = 0.24
LEVELS = 32
LON = 2304
ROWS = 16
DEST = 16
COLS = 144
LANES = 128
VM = pl.BlockSpec(memory_space=pltpu.VMEM)
ANY = pl.BlockSpec(memory_space=pl.ANY)
HB = pl.BlockSpec(memory_space=pltpu.HBM)
PARAMS = pltpu.CompilerParams(vmem_limit_bytes=24 * 1024 * 1024)


def lane_ids(rows):
    return lax.broadcasted_iota(jnp.int32, (rows, LANES), 1)


def row_ids(rows):
    return lax.broadcasted_iota(jnp.int32, (rows, LON), 0)


def courant(pair_sum):
    return courant_max * jnp.tanh(0.5 * pair_sum)


def upwind(flow, before, after):
    return jnp.maximum(flow, 0.0) * before + jnp.minimum(flow, 0.0) * after


def east_roll(x):
    return pltpu.roll(x, 1, 1)


def west_roll(x):
    return pltpu.roll(x, LON - 1, 1)


def zonal(east, mass):
    flux = upwind(east, east_roll(mass), mass)
    return flux - west_roll(flux)


def edge_kernel(tracer, thickness, wind_u, wind_v, to_first, to_second, fetched, sems):
    copies = [
        pltpu.make_async_copy(
            ref.at[level, pl.ds(14 * end, 2), :],
            fetched.at[slot, pl.ds(6 - 4 * level if end else 4 * level, 2), :],
            sems.at[4 * slot + 2 * level + end],
        )
        for slot, ref in enumerate((tracer, thickness, wind_u, wind_v))
        for level in range(2)
        for end in range(2)
    ]
    for copy in copies:
        copy.start()
    for copy in copies:
        copy.wait()
    tracer, layer, u, v = [fetched[slot] for slot in range(4)]
    mass = tracer * layer
    east = courant(east_roll(u) + u)
    north = courant(v + pltpu.roll(v, 7, 0))
    odd = lax.rem(row_ids(8), 2) == 1

    def partial(m):
        flux = upwind(north, m, pltpu.roll(m, 7, 0))
        return m + zonal(east, m) + jnp.where(odd, pltpu.roll(flux, 1, 0), -flux)

    values = (v, mass, layer, partial(mass), partial(layer))
    odd_lat = lax.rem(lax.axis_index("lat"), 2) == 1
    north_first = jnp.broadcast_to(odd_lat, (1, LON))
    for slot, value in enumerate(values):
        for level in range(2):
            south = value[4 * level : 4 * level + 1]
            north_row = value[7 - 4 * level : 8 - 4 * level]
            to_first[slot, level : level + 1, :] = jnp.where(north_first, north_row, south)
            to_second[slot, level : level + 1, :] = jnp.where(north_first, south, north_row)


def first_kernel(tracer, thickness, wind_u, wind_v, send, kept, edges, held):
    row = row_ids(ROWS)
    for level in range(2):
        u, v, layer = wind_u[level], wind_v[level], thickness[level]
        mass = tracer[level] * layer
        east = courant(east_roll(u) + u)
        north = jnp.where(row == 0, 0.0, courant(pltpu.roll(v, 1, 0) + v))
        low, high = slice(4 * level, 4 * level + 2), slice(6 - 4 * level, 8 - 4 * level)

        def keep(slot, value):
            kept[slot, low, :] = value[0:2]
            kept[slot, high, :] = value[14:16]

        keep(0, v)
        keep(5, east)
        keep(7, u)
        kept[6, low, :] = jnp.broadcast_to(-jnp.maximum(north[1:2], 0.0), (2, LON))
        kept[6, high, :] = jnp.broadcast_to(jnp.minimum(north[15:16], 0.0), (2, LON))
        done = []
        for slot, m in enumerate((mass, layer)):
            keep(1 + slot, m)
            for substep in range(2):
                flux = upwind(north, pltpu.roll(m, 1, 0), m)
                above = jnp.where(row == ROWS - 1, 0.0, pltpu.roll(flux, ROWS - 1, 0))
                m = m + zonal(east, m) + flux - above
                if substep == 0:
                    keep(3 + slot, m)
            edges[slot, low, :] = m[0:2]
            edges[slot, high, :] = m[14:16]
            done.append(m)
        mass, layer = done
        for field, m in enumerate((mass, layer * u, layer * v, layer)):
            held[field, level] = m
    lane = lane_ids(ROWS)
    lane8 = lane_ids(8)
    for dest in range(DEST):
        tile = dest + dest // 8
        shift = 16 * (dest % 8)
        low = slice(tile * LANES, (tile + 1) * LANES)
        high = slice((tile + 1) * LANES, (tile + 2) * LANES)
        for level in range(2):
            packed = None
            for field in range(4):
                here = held[field, level, :, low]
                after = held[field, level, :, high]
                block = here if shift == 0 else jnp.where(lane >= shift, here, after)
                start = (field * 2 + level) * ROWS
                send[dest, start : start + ROWS, :] = block
                for half in range(2):
                    part = after[8 * half : 8 * half + 8]
                    part = pltpu.roll(part, 2, 0) if half else part
                    place = 32 * field + 16 * half
                    part = pltpu.roll(part, (place - shift) % LANES, 1)
                    packed = part if packed is None else jnp.where(lane8 >= place, part, packed)
            send[dest, 128 + 8 * level : 136 + 8 * level, :] = packed


def second_kernel(first_halo, second_halo, kept, edges, sent, send, held):
    lat = lax.axis_index("lat")
    row = lax.rem(row_ids(8), 4)
    upper = row >= 2
    outer = (row == 0) | (row == 3)
    even = jnp.broadcast_to(lax.rem(lat, 2) == 0, (1, LON))
    south_open = jnp.where(lat > 0, 1.0, 0.0)
    north_open = jnp.where(lat < lax.axis_size("lat") - 1, 1.0, 0.0)
    open_face = jnp.where(upper, north_open, south_open)

    def halo(slot):
        south, north = [], []
        for level in range(2):
            one = first_halo[slot, level : level + 1, :]
            two = second_halo[slot, level : level + 1, :]
            south.append(jnp.where(even, one, two))
            north.append(jnp.where(even, two, one))
        rows = [jnp.where(upper[0:4], north[1 - level], south[level]) for level in range(2)]
        return jnp.concatenate(rows, axis=0)

    v, east, inner = kept[0], kept[5], kept[6]
    flow = open_face * courant(v + halo(0))
    sign = jnp.where(upper, -1.0, 1.0)
    done = []
    for slot in range(2):
        m, m_beyond = kept[1 + slot], halo(1 + slot)
        partial, beyond = kept[3 + slot], halo(3 + slot)
        flux = upwind(flow, jnp.where(upper, m, m_beyond), jnp.where(upper, m_beyond, m))
        change = jnp.where(outer, sign * flux, 0.0)
        partial = partial + change
        beyond = beyond - change
        flux = upwind(flow, jnp.where(upper, partial, beyond), jnp.where(upper, beyond, partial))
        carried = inner * change
        gain = change + zonal(east, change) + carried + sign * flux
        passed = jnp.where(row == 1, pltpu.roll(carried, 1, 0), pltpu.roll(carried, 7, 0))
        done.append(edges[slot] + jnp.where(outer, gain, -passed))
    mass, layer = done
    for field, m in enumerate((mass, layer * kept[7], layer * v, layer)):
        held[field] = m
    lane = lane_ids(8)
    upper_half = lax.rem(lane, 32) >= 16
    place = lax.broadcasted_iota(jnp.int32, (8, LANES), 0)
    low_ends, high_ends = place < 2, place >= 6
    for dest in range(DEST):
        tile = dest + dest // 8
        shift = 16 * (dest % 8)
        low = slice(tile * LANES, (tile + 1) * LANES)
        high = slice((tile + 1) * LANES, (tile + 2) * LANES)
        halves = [None, None]
        for field in range(4):
            here, after = held[field, :, low], held[field, :, high]
            block = here if shift == 0 else jnp.where(lane >= shift, here, after)
            for level in range(2):
                ends = pltpu.roll(block, 4, 0) if level else block
                start = (field * 2 + level) * ROWS
                rows = sent[dest, start : start + 8, :]
                send[dest, start : start + 8, :] = jnp.where(low_ends, ends, rows)
                rows = sent[dest, start + 8 : start + 16, :]
                send[dest, start + 8 : start + 16, :] = jnp.where(high_ends, ends, rows)
            for half in range(2):
                part = pltpu.roll(after, (32 * field + 16 * half - shift) % LANES, 1)
                halves[half] = jnp.where(lane >= 32 * field, part, halves[half]) if field else part
        first, last = halves
        for level, ends in enumerate(
            (
                jnp.where(upper_half, pltpu.roll(last, 2, 0), first),
                jnp.where(upper_half, pltpu.roll(last, 6, 0), pltpu.roll(first, 4, 0)),
            )
        ):
            start = 128 + 8 * level
            rows = sent[dest, start : start + 8, :]
            send[dest, start : start + 8, :] = jnp.where(low_ends, ends, rows)


def factor_kernel(offsets, coupling, factors_main, factors_rest):
    shift = 16 * lax.rem(lax.axis_index("lev"), 8)
    half = lax.rem(lane_ids(8), 32) >= 16

    def main(ref, k):
        return pltpu.roll(ref[k, :, 0:LANES], shift, 1)

    def rest(ref, k):
        part = ref[k, :, LANES:COLS]
        both = jnp.concatenate([part[0:8], part[8:16]], axis=1)
        all_fields = jnp.concatenate([both, both, both, both], axis=1)
        return jnp.where(half, pltpu.roll(all_fields, 2, 0), all_fields)

    for load, factors, shape in (
        (main, factors_main, (ROWS, LANES)),
        (rest, factors_rest, (8, LANES)),
    ):
        low = jnp.zeros(shape, jnp.float32)
        back = jnp.zeros(shape, jnp.float32)
        for k in range(LEVELS):
            choose = load(offsets, k)
            high = load(coupling, k) if k < LEVELS - 1 else jnp.zeros(shape, jnp.float32)
            scale = 1.0 / (1.0 + low + high - low * back)
            back = high * scale
            factors[0, k] = jnp.where(choose == 0, -scale, scale)
            factors[1, k] = low * scale
            factors[2, k] = jnp.where(choose == 2, -back, back)
            low = high


def column_kernel(received, factors_main, factors_rest, send):
    lane = lane_ids(8)

    def main(k):
        base = (k % 2) * ROWS
        return [received[k // 2, base + 32 * f : base + 32 * f + ROWS, :] for f in range(4)]

    def rest(k):
        base = 128 + 8 * (k % 2)
        return received[k // 2, base : base + 8, :]

    def picked(below, above, sums):
        return jnp.where(below, sums[0], jnp.where(above, sums[2], sums[1]))

    solve_main = [jnp.zeros((ROWS, LANES), jnp.float32)] * 3
    solve_rest = jnp.zeros((8, LANES), jnp.float32)
    main_here, rest_here = main(0), rest(0)
    main_sums, rest_sums = [], []

    def push(k):
        nonlocal main_here, rest_here
        main_next, rest_next = main(k + 1), rest(k + 1)
        main_sums.append([a + b for a, b in zip(main_here, main_next)])
        rest_sums.append(rest_here + rest_next)
        main_here, rest_here = main_next, rest_next

    push(0)
    for k in range(LEVELS):
        if k + 1 < LEVELS - 1:
            push(k + 1)
        three = [max(k - 1, 0), min(k, LEVELS - 2), min(k + 1, LEVELS - 2)]
        scale = factors_main[0, k]
        below, above = scale < 0.0, factors_main[2, k] < 0.0
        values = [picked(below, above, [main_sums[i][f] for i in three]) for f in range(4)]
        weight = jnp.abs(scale) / values[3]
        low = factors_main[1, k]
        solve_main = [values[f] * weight + low * solve_main[f] for f in range(3)]
        for f in range(3):
            base = (f * 2 + k % 2) * ROWS
            send[k // 2, base : base + ROWS, :] = solve_main[f]
        scale = factors_rest[0, k]
        below, above = scale < 0.0, factors_rest[2, k] < 0.0
        value = picked(below, above, [rest_sums[i] for i in three])
        total = jnp.where(lane >= 64, pltpu.roll(value, 96, 1), pltpu.roll(value, 32, 1))
        total = jnp.where(lane >= 32, jnp.where(lane >= 64, total, pltpu.roll(value, 64, 1)), total)
        solve_rest = value * (jnp.abs(scale) / total) + factors_rest[1, k] * solve_rest
        base = 96 + 8 * (k % 2)
        send[k // 2, base : base + 8, :] = solve_rest
    for k in range(LEVELS - 2, -1, -1):
        back = jnp.abs(factors_main[2, k])
        for f in range(3):
            base = (f * 2 + k % 2) * ROWS
            solve_main[f] = send[k // 2, base : base + ROWS, :] + back * solve_main[f]
            send[k // 2, base : base + ROWS, :] = solve_main[f]
        base = 96 + 8 * (k % 2)
        solve_rest = send[k // 2, base : base + 8, :] + jnp.abs(factors_rest[2, k]) * solve_rest
        send[k // 2, base : base + 8, :] = solve_rest


def unpack_kernel(received, tracer_out, u_out, v_out, whole, sems):
    lane = lane_ids(ROWS)
    copies = []
    for field, out in enumerate((tracer_out, u_out, v_out)):
        for level in range(2):
            base = (field * 2 + level) * ROWS
            for tile in range(LON // LANES):
                source = tile if tile < 8 else tile - 1
                fresh = tile != 8 and tile != 17
                shift = 16 * (source % 8) if fresh else LANES
                value = received[source, base : base + ROWS, :] if fresh else None
                if shift > 0:
                    last = source - 1 if fresh else (7 if tile == 8 else 15)
                    place = shift - 16
                    packed = received[last, 96 + 8 * level : 104 + 8 * level, :]
                    start = place - 32 * field
                    rest = jnp.concatenate(
                        [
                            pltpu.roll(packed, start % LANES, 1),
                            pltpu.roll(pltpu.roll(packed, 6, 0), (start - 16) % LANES, 1),
                        ],
                        axis=0,
                    )
                    old = received[last, base : base + ROWS, :]
                    old = jnp.where(lane >= place, rest, old) if place > 0 else rest
                    value = jnp.where(lane >= shift, value, old) if fresh else old
                whole[field, level, :, tile * LANES : (tile + 1) * LANES] = value
            copy = pltpu.make_async_copy(
                whole.at[field, level], out.at[level], sems.at[2 * field + level]
            )
            copy.start()
            copies.append(copy)
    for copy in copies:
        copy.wait()


def call(kernel, in_specs, outs, scratch=(), aliases=None, flops=1000000, nbytes=3000000):
    return pl.pallas_call(
        kernel,
        in_specs=in_specs,
        out_specs=[spec for spec, _ in outs],
        out_shape=[jax.ShapeDtypeStruct(shape, jnp.float32) for _, shape in outs],
        scratch_shapes=scratch,
        input_output_aliases=aliases or {},
        compiler_params=PARAMS,
        cost_estimate=pl.CostEstimate(flops=flops, bytes_accessed=nbytes, transcendentals=0),
    )


def local(tracer, thickness, wind_u, wind_v, offsets, coupling):
    f32 = jnp.float32
    lat_count = lax.axis_size("lat")
    slab = (2, ROWS, LON)
    halo = (5, 2, LON)
    chunks = (DEST, 144, LANES)

    def transposed(block):
        return lax.all_to_all(block, "lev", split_axis=0, concat_axis=0, tiled=True)

    fields = [
        pltpu.with_memory_space_constraint(x, pltpu.HBM)
        for x in (tracer, thickness, wind_u, wind_v)
    ]
    to_first, to_second = call(
        edge_kernel,
        [HB] * 4,
        [(VM, halo), (VM, halo)],
        scratch=[pltpu.VMEM((4, 8, LON), f32), pltpu.SemaphoreType.DMA((16,))],
    )(*fields)
    lev_count = lax.axis_size("lev")
    moves = []
    for start in (1, 0):
        pairs = [(i, i + 1) for i in range(start, lat_count - 1, 2)]
        lats = dict(pairs + [(b, a) for a, b in pairs])
        moves.append(
            [
                (lat * lev_count + lev, lats[lat] * lev_count + lev if lat in lats else lat * lev_count + (lev ^ 1))
                for lat in range(lat_count)
                for lev in range(lev_count)
            ]
        )
    first_halo, second_halo = [
        lax.ppermute(rows, ("lat", "lev"), move) for rows, move in zip((to_first, to_second), moves)
    ]
    send, kept, edges = call(
        first_kernel,
        [VM] * 4,
        [(VM, chunks), (VM, (8, 8, LON)), (VM, (2, 8, LON))],
        scratch=[pltpu.VMEM((4,) + slab, f32)],
    )(tracer, thickness, wind_u, wind_v)
    factors = call(
        factor_kernel,
        [VM, VM],
        [(VM, (3, LEVELS, ROWS, LANES)), (VM, (3, LEVELS, 8, LANES))],
    )(offsets, coupling)
    edges, *factors = lax.optimization_barrier((edges, *factors))
    (send,) = call(
        second_kernel,
        [VM] * 5,
        [(VM, chunks)],
        scratch=[pltpu.VMEM((4, 8, LON), f32)],
    )(first_halo, second_halo, kept, edges, send)
    received = transposed(send)
    (back,) = call(column_kernel, [VM] * 3, [(VM, (DEST, 112, LANES))])(received, *factors)
    returned = transposed(back)
    return tuple(
        call(
            unpack_kernel,
            [VM],
            [(ANY, slab)] * 3,
            scratch=[pltpu.VMEM((3,) + slab, f32), pltpu.SemaphoreType.DMA((6,))],
        )(returned)
    )


def solution(mesh):
    return jax.shard_map(
        local,
        mesh=mesh,
        in_specs=(
            P("lev", "lat", None),
            P("lev", "lat", None),
            P("lev", "lat", None),
            P("lev", "lat", None),
            P(None, "lat", "lev"),
            P(None, "lat", "lev"),
        ),
        out_specs=(P("lev", "lat", None), P("lev", "lat", None), P("lev", "lat", None)),
        check_vma=False,
    )
```

```python
import jax
import jax.numpy as jnp
from jax import lax
from jax.experimental import pallas as pl
from jax.experimental.pallas import tpu as pltpu
from jax.sharding import PartitionSpec as P

courant_max = 0.24
LEVELS = 32
LON = 2304
ROWS = 16
DEST = 16
COLS = 144
LANES = 128
VM = pl.BlockSpec(memory_space=pltpu.VMEM)
ANY = pl.BlockSpec(memory_space=pl.ANY)
HB = pl.BlockSpec(memory_space=pltpu.HBM)
PARAMS = pltpu.CompilerParams(vmem_limit_bytes=24 * 1024 * 1024)


def lane_ids(rows):
    return lax.broadcasted_iota(jnp.int32, (rows, LANES), 1)


def row_ids(rows):
    return lax.broadcasted_iota(jnp.int32, (rows, LON), 0)


def courant(pair_sum):
    return courant_max * jnp.tanh(0.5 * pair_sum)


def upwind(flow, before, after):
    return jnp.maximum(flow, 0.0) * before + jnp.minimum(flow, 0.0) * after


def east_roll(x):
    return pltpu.roll(x, 1, 1)


def west_roll(x):
    return pltpu.roll(x, LON - 1, 1)


def zonal(east, mass):
    flux = upwind(east, east_roll(mass), mass)
    return flux - west_roll(flux)


def edge_kernel(tracer, thickness, wind_u, wind_v, to_first, to_second, fetched, sems):
    copies = [
        pltpu.make_async_copy(
            ref.at[level, pl.ds(14 * end, 2), :],
            fetched.at[slot, pl.ds(6 - 4 * level if end else 4 * level, 2), :],
            sems.at[4 * slot + 2 * level + end],
        )
        for slot, ref in enumerate((tracer, thickness, wind_u, wind_v))
        for level in range(2)
        for end in range(2)
    ]
    for copy in copies:
        copy.start()
    for copy in copies:
        copy.wait()
    tracer, layer, u, v = [fetched[slot] for slot in range(4)]
    mass = tracer * layer
    east = courant(east_roll(u) + u)
    north = courant(v + pltpu.roll(v, 7, 0))
    odd = lax.rem(row_ids(8), 2) == 1

    def partial(m):
        flux = upwind(north, m, pltpu.roll(m, 7, 0))
        return m + zonal(east, m) + jnp.where(odd, pltpu.roll(flux, 1, 0), -flux)

    values = (v, mass, layer, partial(mass), partial(layer))
    odd_lat = lax.rem(lax.axis_index("lat"), 2) == 1
    north_first = jnp.broadcast_to(odd_lat, (1, LON))
    for slot, value in enumerate(values):
        for level in range(2):
            south = value[4 * level : 4 * level + 1]
            north_row = value[7 - 4 * level : 8 - 4 * level]
            to_first[slot, level : level + 1, :] = jnp.where(north_first, north_row, south)
            to_second[slot, level : level + 1, :] = jnp.where(north_first, south, north_row)


def first_kernel(tracer, thickness, wind_u, wind_v, send, kept, edges, held):
    row = row_ids(ROWS)
    for level in range(2):
        u, v, layer = wind_u[level], wind_v[level], thickness[level]
        mass = tracer[level] * layer
        east = courant(east_roll(u) + u)
        north = jnp.where(row == 0, 0.0, courant(pltpu.roll(v, 1, 0) + v))
        low, high = slice(4 * level, 4 * level + 2), slice(6 - 4 * level, 8 - 4 * level)

        def keep(slot, value):
            kept[slot, low, :] = value[0:2]
            kept[slot, high, :] = value[14:16]

        keep(0, v)
        keep(5, east)
        keep(7, u)
        kept[6, low, :] = jnp.broadcast_to(-jnp.maximum(north[1:2], 0.0), (2, LON))
        kept[6, high, :] = jnp.broadcast_to(jnp.minimum(north[15:16], 0.0), (2, LON))
        done = []
        for slot, m in enumerate((mass, layer)):
            keep(1 + slot, m)
            for substep in range(2):
                flux = upwind(north, pltpu.roll(m, 1, 0), m)
                above = jnp.where(row == ROWS - 1, 0.0, pltpu.roll(flux, ROWS - 1, 0))
                m = m + zonal(east, m) + flux - above
                if substep == 0:
                    keep(3 + slot, m)
            edges[slot, low, :] = m[0:2]
            edges[slot, high, :] = m[14:16]
            done.append(m)
        mass, layer = done
        for field, m in enumerate((mass, layer * u, layer * v, layer)):
            held[field, level] = m
    lane = lane_ids(ROWS)
    lane8 = lane_ids(8)
    for dest in range(DEST):
        tile = dest + dest // 8
        shift = 16 * (dest % 8)
        low = slice(tile * LANES, (tile + 1) * LANES)
        high = slice((tile + 1) * LANES, (tile + 2) * LANES)
        for level in range(2):
            packed = None
            for field in range(4):
                here = held[field, level, :, low]
                after = held[field, level, :, high]
                block = here if shift == 0 else jnp.where(lane >= shift, here, after)
                start = (field * 2 + level) * ROWS
                send[dest, start : start + ROWS, :] = block
                for half in range(2):
                    part = after[8 * half : 8 * half + 8]
                    part = pltpu.roll(part, 2, 0) if half else part
                    place = 32 * field + 16 * half
                    part = pltpu.roll(part, (place - shift) % LANES, 1)
                    packed = part if packed is None else jnp.where(lane8 >= place, part, packed)
            send[dest, 128 + 8 * level : 136 + 8 * level, :] = packed


def second_kernel(first_halo, second_halo, kept, edges, sent, send, held):
    lat = lax.axis_index("lat")
    row = lax.rem(row_ids(8), 4)
    upper = row >= 2
    outer = (row == 0) | (row == 3)
    even = jnp.broadcast_to(lax.rem(lat, 2) == 0, (1, LON))
    south_open = jnp.where(lat > 0, 1.0, 0.0)
    north_open = jnp.where(lat < lax.axis_size("lat") - 1, 1.0, 0.0)
    open_face = jnp.where(upper, north_open, south_open)

    def halo(slot):
        south, north = [], []
        for level in range(2):
            one = first_halo[slot, level : level + 1, :]
            two = second_halo[slot, level : level + 1, :]
            south.append(jnp.where(even, one, two))
            north.append(jnp.where(even, two, one))
        rows = [jnp.where(upper[0:4], north[1 - level], south[level]) for level in range(2)]
        return jnp.concatenate(rows, axis=0)

    v, east, inner = kept[0], kept[5], kept[6]
    flow = open_face * courant(v + halo(0))
    sign = jnp.where(upper, -1.0, 1.0)
    done = []
    for slot in range(2):
        m, m_beyond = kept[1 + slot], halo(1 + slot)
        partial, beyond = kept[3 + slot], halo(3 + slot)
        flux = upwind(flow, jnp.where(upper, m, m_beyond), jnp.where(upper, m_beyond, m))
        change = jnp.where(outer, sign * flux, 0.0)
        partial = partial + change
        beyond = beyond - change
        flux = upwind(flow, jnp.where(upper, partial, beyond), jnp.where(upper, beyond, partial))
        carried = inner * change
        gain = change + zonal(east, change) + carried + sign * flux
        passed = jnp.where(row == 1, pltpu.roll(carried, 1, 0), pltpu.roll(carried, 7, 0))
        done.append(edges[slot] + jnp.where(outer, gain, -passed))
    mass, layer = done
    for field, m in enumerate((mass, layer * kept[7], layer * v, layer)):
        held[field] = m
    lane = lane_ids(8)
    upper_half = lax.rem(lane, 32) >= 16
    place = lax.broadcasted_iota(jnp.int32, (8, LANES), 0)
    low_ends, high_ends = place < 2, place >= 6
    for dest in range(DEST):
        tile = dest + dest // 8
        shift = 16 * (dest % 8)
        low = slice(tile * LANES, (tile + 1) * LANES)
        high = slice((tile + 1) * LANES, (tile + 2) * LANES)
        halves = [None, None]
        for field in range(4):
            here, after = held[field, :, low], held[field, :, high]
            block = here if shift == 0 else jnp.where(lane >= shift, here, after)
            for level in range(2):
                ends = pltpu.roll(block, 4, 0) if level else block
                start = (field * 2 + level) * ROWS
                rows = sent[dest, start : start + 8, :]
                send[dest, start : start + 8, :] = jnp.where(low_ends, ends, rows)
                rows = sent[dest, start + 8 : start + 16, :]
                send[dest, start + 8 : start + 16, :] = jnp.where(high_ends, ends, rows)
            for half in range(2):
                part = pltpu.roll(after, (32 * field + 16 * half - shift) % LANES, 1)
                halves[half] = jnp.where(lane >= 32 * field, part, halves[half]) if field else part
        first, last = halves
        for level, ends in enumerate(
            (
                jnp.where(upper_half, pltpu.roll(last, 2, 0), first),
                jnp.where(upper_half, pltpu.roll(last, 6, 0), pltpu.roll(first, 4, 0)),
            )
        ):
            start = 128 + 8 * level
            rows = sent[dest, start : start + 8, :]
            send[dest, start : start + 8, :] = jnp.where(low_ends, ends, rows)


def factor_kernel(offsets, coupling, factors_main, factors_rest):
    shift = 16 * lax.rem(lax.axis_index("lev"), 8)
    half = lax.rem(lane_ids(8), 32) >= 16

    def main(ref, k):
        return pltpu.roll(ref[k, :, 0:LANES], shift, 1)

    def rest(ref, k):
        part = ref[k, :, LANES:COLS]
        both = jnp.concatenate([part[0:8], part[8:16]], axis=1)
        all_fields = jnp.concatenate([both, both, both, both], axis=1)
        return jnp.where(half, pltpu.roll(all_fields, 2, 0), all_fields)

    for load, factors, shape in (
        (main, factors_main, (ROWS, LANES)),
        (rest, factors_rest, (8, LANES)),
    ):
        low = jnp.zeros(shape, jnp.float32)
        back = jnp.zeros(shape, jnp.float32)
        for k in range(LEVELS):
            choose = load(offsets, k)
            high = load(coupling, k) if k < LEVELS - 1 else jnp.zeros(shape, jnp.float32)
            scale = 1.0 / (1.0 + low + high - low * back)
            back = high * scale
            factors[0, k] = jnp.where(choose == 0, -scale, scale)
            factors[1, k] = low * scale
            factors[2, k] = jnp.where(choose == 2, -back, back)
            low = high


def column_kernel(received, factors_main, factors_rest, send):
    lane = lane_ids(8)

    def main(k):
        base = (k % 2) * ROWS
        return [received[k // 2, base + 32 * f : base + 32 * f + ROWS, :] for f in range(4)]

    def rest(k):
        base = 128 + 8 * (k % 2)
        return received[k // 2, base : base + 8, :]

    def picked(below, above, sums):
        return jnp.where(below, sums[0], jnp.where(above, sums[2], sums[1]))

    solve_main = [jnp.zeros((ROWS, LANES), jnp.float32)] * 3
    solve_rest = jnp.zeros((8, LANES), jnp.float32)
    main_here, rest_here = main(0), rest(0)
    main_sums, rest_sums = [], []

    def push(k):
        nonlocal main_here, rest_here
        main_next, rest_next = main(k + 1), rest(k + 1)
        main_sums.append([a + b for a, b in zip(main_here, main_next)])
        rest_sums.append(rest_here + rest_next)
        main_here, rest_here = main_next, rest_next

    push(0)
    for k in range(LEVELS):
        if k + 1 < LEVELS - 1:
            push(k + 1)
        three = [max(k - 1, 0), min(k, LEVELS - 2), min(k + 1, LEVELS - 2)]
        scale = factors_main[0, k]
        below, above = scale < 0.0, factors_main[2, k] < 0.0
        values = [picked(below, above, [main_sums[i][f] for i in three]) for f in range(4)]
        weight = jnp.abs(scale) / values[3]
        low = factors_main[1, k]
        solve_main = [values[f] * weight + low * solve_main[f] for f in range(3)]
        for f in range(3):
            base = (f * 2 + k % 2) * ROWS
            send[k // 2, base : base + ROWS, :] = solve_main[f]
        scale = factors_rest[0, k]
        below, above = scale < 0.0, factors_rest[2, k] < 0.0
        value = picked(below, above, [rest_sums[i] for i in three])
        total = jnp.where(lane >= 64, pltpu.roll(value, 96, 1), pltpu.roll(value, 32, 1))
        total = jnp.where(lane >= 32, jnp.where(lane >= 64, total, pltpu.roll(value, 64, 1)), total)
        solve_rest = value * (jnp.abs(scale) / total) + factors_rest[1, k] * solve_rest
        base = 96 + 8 * (k % 2)
        send[k // 2, base : base + 8, :] = solve_rest
    for k in range(LEVELS - 2, -1, -1):
        back = jnp.abs(factors_main[2, k])
        for f in range(3):
            base = (f * 2 + k % 2) * ROWS
            solve_main[f] = send[k // 2, base : base + ROWS, :] + back * solve_main[f]
            send[k // 2, base : base + ROWS, :] = solve_main[f]
        base = 96 + 8 * (k % 2)
        solve_rest = send[k // 2, base : base + 8, :] + jnp.abs(factors_rest[2, k]) * solve_rest
        send[k // 2, base : base + 8, :] = solve_rest


def unpack_kernel(received, tracer_out, u_out, v_out, whole, sems):
    lane = lane_ids(ROWS)
    copies = []
    for field, out in enumerate((tracer_out, u_out, v_out)):
        for level in range(2):
            base = (field * 2 + level) * ROWS
            for tile in range(LON // LANES):
                source = tile if tile < 8 else tile - 1
                fresh = tile != 8 and tile != 17
                shift = 16 * (source % 8) if fresh else LANES
                value = received[source, base : base + ROWS, :] if fresh else None
                if shift > 0:
                    last = source - 1 if fresh else (7 if tile == 8 else 15)
                    place = shift - 16
                    packed = received[last, 96 + 8 * level : 104 + 8 * level, :]
                    start = place - 32 * field
                    rest = jnp.concatenate(
                        [
                            pltpu.roll(packed, start % LANES, 1),
                            pltpu.roll(pltpu.roll(packed, 6, 0), (start - 16) % LANES, 1),
                        ],
                        axis=0,
                    )
                    old = received[last, base : base + ROWS, :]
                    old = jnp.where(lane >= place, rest, old) if place > 0 else rest
                    value = jnp.where(lane >= shift, value, old) if fresh else old
                whole[field, level, :, tile * LANES : (tile + 1) * LANES] = value
        copy = pltpu.make_async_copy(whole.at[field], out, sems.at[field])
        copy.start()
        copies.append(copy)
    for copy in copies:
        copy.wait()


def call(kernel, in_specs, outs, scratch=(), aliases=None, flops=1000000, nbytes=3000000):
    return pl.pallas_call(
        kernel,
        in_specs=in_specs,
        out_specs=[spec for spec, _ in outs],
        out_shape=[jax.ShapeDtypeStruct(shape, jnp.float32) for _, shape in outs],
        scratch_shapes=scratch,
        input_output_aliases=aliases or {},
        compiler_params=PARAMS,
        cost_estimate=pl.CostEstimate(flops=flops, bytes_accessed=nbytes, transcendentals=0),
    )


def local(tracer, thickness, wind_u, wind_v, offsets, coupling):
    f32 = jnp.float32
    lat_count = lax.axis_size("lat")
    slab = (2, ROWS, LON)
    halo = (5, 2, LON)
    chunks = (DEST, 144, LANES)

    def transposed(block):
        return lax.all_to_all(block, "lev", split_axis=0, concat_axis=0, tiled=True)

    fields = [
        pltpu.with_memory_space_constraint(x, pltpu.HBM)
        for x in (tracer, thickness, wind_u, wind_v)
    ]
    to_first, to_second = call(
        edge_kernel,
        [HB] * 4,
        [(VM, halo), (VM, halo)],
        scratch=[pltpu.VMEM((4, 8, LON), f32), pltpu.SemaphoreType.DMA((16,))],
    )(*fields)
    lev_count = lax.axis_size("lev")
    moves = []
    for start in (1, 0):
        pairs = [(i, i + 1) for i in range(start, lat_count - 1, 2)]
        lats = dict(pairs + [(b, a) for a, b in pairs])
        moves.append(
            [
                (lat * lev_count + lev, lats[lat] * lev_count + lev if lat in lats else lat * lev_count + (lev ^ 1))
                for lat in range(lat_count)
                for lev in range(lev_count)
            ]
        )
    first_halo, second_halo = [
        lax.ppermute(rows, ("lat", "lev"), move) for rows, move in zip((to_first, to_second), moves)
    ]
    send, kept, edges = call(
        first_kernel,
        [VM] * 4,
        [(VM, chunks), (VM, (8, 8, LON)), (VM, (2, 8, LON))],
        scratch=[pltpu.VMEM((4,) + slab, f32)],
    )(tracer, thickness, wind_u, wind_v)
    factors = call(
        factor_kernel,
        [VM, VM],
        [(VM, (3, LEVELS, ROWS, LANES)), (VM, (3, LEVELS, 8, LANES))],
    )(offsets, coupling)
    edges, *factors = lax.optimization_barrier((edges, *factors))
    (send,) = call(
        second_kernel,
        [VM] * 5,
        [(VM, chunks)],
        scratch=[pltpu.VMEM((4, 8, LON), f32)],
    )(first_halo, second_halo, kept, edges, send)
    received = transposed(send)
    (back,) = call(column_kernel, [VM] * 3, [(VM, (DEST, 112, LANES))])(received, *factors)
    returned = transposed(back)
    return tuple(
        call(
            unpack_kernel,
            [VM],
            [(ANY, slab)] * 3,
            scratch=[pltpu.VMEM((3,) + slab, f32), pltpu.SemaphoreType.DMA((3,))],
        )(returned)
    )


def solution(mesh):
    return jax.shard_map(
        local,
        mesh=mesh,
        in_specs=(
            P("lev", "lat", None),
            P("lev", "lat", None),
            P("lev", "lat", None),
            P("lev", "lat", None),
            P(None, "lat", "lev"),
            P(None, "lat", "lev"),
        ),
        out_specs=(P("lev", "lat", None), P("lev", "lat", None), P("lev", "lat", None)),
        check_vma=False,
    )
```
